512 devices in a mesh: section: 16 (over z, core), expert: 32 (over y, x).
Axes of the slice: x: 4, y: 8, z: 8, core: 2. Of those that a mesh axis runs over, the one named last changes fastest.
Arguments:
- tokens: bfloat16 [192, 4096], P('expert'), may hold values from -6 to 6
- expert_ids: int32 [16, 192, 1], P('section', 'expert'), may hold values from 0 to 3; in each aligned block of 6 rows (0 to 5, 6 to 11, ..., all dimensions but the last counted through in order) at most 2 rows name the same one
- gate_scale: float32 [16, 192], P('section', 'expert'), may hold values from 0.3 to 1
- norm_gain: float32 [16, 4096], P('section'), may hold values from 0.5 to 1.5
- w_gate: bfloat16 [16, 4096, 4096], P('section', None, 'expert'), may hold values from -0.09375 to 0.09375
- w_up: bfloat16 [16, 4096, 4096], P('section', None, 'expert'), may hold values from -0.09375 to 0.09375
- w_down: bfloat16 [16, 4096, 4096], P('section', 'expert'), may hold values from -0.1875 to 0.1875
Outputs:
- section_out: bfloat16 [16, 192, 4096], P('section', 'expert')
The draws below stay inside these ranges and needn't reach their ends.
Inputs may be any that keep to these rules, and one draw needn't show every extreme that they name: `expert_ids`: within each layer, the 6 tokens of one index of expert choose any one expert at most 2 times.
All inputs are finite; a program needn't handle non-finite values.
Results may differ from the reference program's by a relative error of at most 0.035.
Values may be sent and summed in bfloat16 or wider, within the bound.
A program may use at most 64 MiB of HBM per device.

```python
import math
import jax
import jax.numpy as jnp
import numpy as np
from jax import lax

D = 4096
FF = 1024
EXPERTS = 4
TOP = 1
TOK_DEV = 6
CAP = 2
SECTIONS = 16
TOKENS = 192
N_EXPERT = 32


def steps_of(key, extent, cuts, low, top_value):
    def one(axis_at, shards_of):
        draws = jax.random.uniform(jax.random.fold_in(jax.random.fold_in(key, 6), axis_at), (shards_of,), jnp.float32, low / len(cuts), top_value / len(cuts))
        return jnp.repeat(jnp.exp(draws), extent[axis_at] // shards_of).reshape((-1,) + (1,) * (len(extent) - axis_at - 1))

    level = one(*cuts[0])
    for cut in cuts[1:]:
        level = level * one(*cut)
    return level


def deal_out(own_key, own, number, rows, count, top, limit, slope):
    ranking = jax.random.permutation(own_key, count)
    packed, common = load_shares(count, rows * top, limit, slope, True), load_shares(count, rows * top, limit, slope, False)
    places = jnp.arange(count)

    def named(tallies, offset_by):
        used = int((tallies > 0).sum())
        fixed = max(1, used // 4)
        passed = fixed + (places - fixed + offset_by * (used - fixed)) % max(1, count - fixed)
        return jnp.zeros((count,), jnp.int32).at[ranking[jnp.where(places < fixed, places, passed)]].set(jnp.asarray(tallies, jnp.int32))

    tallies = jnp.where(number % 4 == 0, named(packed, number // 4), named(common, number - number // 4 - 1))
    mixed = jax.random.permutation(jax.random.fold_in(own, 3), count)
    donor, taker = mixed[0:count // 2 * 2:2], mixed[1:count // 2 * 2:2]
    margin = jnp.minimum(tallies[donor] - 1, limit - tallies[taker]) // 2
    margin = jnp.where((donor == ranking[0]) | (taker == ranking[0]) | (tallies[taker] == 0), 0, jnp.maximum(margin, 0))
    passed = jax.random.randint(jax.random.fold_in(own, 4), (count // 2,), 0, 1 << 20) % (margin + 1)
    tallies = tallies.at[donor].add(-passed).at[taker].add(passed)
    labels = jnp.searchsorted(jnp.cumsum(tallies), jnp.arange(rows * top), side="right").astype(jnp.int32)
    grid = labels.reshape(top, rows).T
    grid = grid[jax.random.permutation(jax.random.fold_in(own, 1), rows)]
    offset_by = jax.random.randint(jax.random.fold_in(own, 2), (rows, 1), 0, top)
    return jnp.take_along_axis(grid, (jnp.arange(top)[None, :] + offset_by) % top, axis=1)


def load_shares(amount, total, limit, skew, full):
    weights = [(1 << 20) // math.isqrt(standing ** skew) + 1 for standing in range(1, amount + 1)]
    largest = limit if full else min(limit, max(-(-total // amount), total * weights[0] // sum(weights)))
    least = 1 if total - largest >= amount - 1 else 0
    counts, rest = [largest] + [least] * (amount - 1), total - largest - least * (amount - 1)
    while rest > 0:
        free = [i for i in range(1, amount) if counts[i] < largest] or [i for i in range(1, amount) if counts[i] < limit]
        whole, remaining = sum([weights[i] for i in free]), rest
        for i in free:
            addition = min(limit - counts[i], max(1, remaining * weights[i] // whole), rest)
            counts[i] = counts[i] + addition
            rest = rest - addition
    return np.array(counts)


def normal_values(stream_key, dims, scale, reach, split=(), kind=jnp.bfloat16):
    loudness = steps_of(stream_key, dims, split, -0.22, 0.18) if split else 1.0
    result = jax.random.normal(stream_key, dims, jnp.float32) * scale * loudness
    return jnp.minimum(jnp.maximum(result, -reach), reach).astype(kind)


def setup_inputs(seed: int = 0) -> dict:
    streams_of = jax.random.split(jax.random.key(seed), 8)
    tokens = normal_values(streams_of[0], (TOKENS, D), 1.0, 6.0, ((0, 32),))
    expert_ids_keys = jax.random.split(jax.random.fold_in(streams_of[1], 1), SECTIONS * TOKENS // TOK_DEV)
    expert_ids_turns = jax.random.permutation(jax.random.fold_in(streams_of[1], 3), SECTIONS * TOKENS // TOK_DEV)
    expert_ids = jax.vmap(lambda own, number: deal_out(jax.random.fold_in(streams_of[1], 2), own, number, TOK_DEV, EXPERTS, TOP, CAP, 2))(expert_ids_keys, expert_ids_turns).reshape((SECTIONS, TOKENS, TOP))
    gate_scale = jnp.clip(0.3 + 0.7 * jax.random.uniform(streams_of[2], (SECTIONS, TOKENS), jnp.float32) ** steps_of(streams_of[2], (SECTIONS, TOKENS), ((0, 16), (1, 32)), -0.2, 0.2), 0.3, 1.0)
    norm_gain = jnp.clip(1.0 + 0.1 * jax.random.normal(streams_of[3], (SECTIONS, D), jnp.float32), 0.5, 1.5)
    w_gate = normal_values(streams_of[4], (SECTIONS, D, EXPERTS * FF), D ** -0.5, 0.09375, ((0, 16), (2, 32)))
    w_up = normal_values(streams_of[5], (SECTIONS, D, EXPERTS * FF), D ** -0.5, 0.09375, ((0, 16), (2, 32)))
    w_down = normal_values(streams_of[6], (SECTIONS, EXPERTS * FF, D), FF ** -0.5, 0.1875, ((0, 16), (1, 32)))
    return dict(tokens=tokens, expert_ids=expert_ids, gate_scale=gate_scale, norm_gain=norm_gain, w_gate=w_gate, w_up=w_up, w_down=w_down)


def norm_rows(state, gain):
    values = state.astype(jnp.float32)
    scale = lax.rsqrt(lax.optimization_barrier(jnp.mean(values * values, axis=-1, keepdims=True)) + 1e-06)
    return (values * scale * gain.astype(jnp.float32)).astype(jnp.bfloat16)

def reference(tokens, expert_ids, gate_scale, norm_gain, w_gate, w_up, w_down):
    group = N_EXPERT // EXPERTS
    width = FF // group
    state = tokens
    results = []
    for layer in range(SECTIONS):
        normed = norm_rows(state, norm_gain[layer])
        chosen = expert_ids[layer, :, 0]
        total = jnp.zeros((TOKENS, D), jnp.float32)
        for expert in range(EXPERTS):
            first = expert * FF
            gate = jnp.dot(normed, w_gate[layer, :, first:first + FF], preferred_element_type=jnp.float32)
            upward = jnp.dot(normed, w_up[layer, :, first:first + FF], preferred_element_type=jnp.float32)
            hidden = (jax.nn.silu(gate) * upward).astype(jnp.bfloat16)
            blocks = hidden.reshape(TOKENS, group, width).astype(jnp.float32)
            downs = w_down[layer, first:first + FF, :].reshape(group, width, D).astype(jnp.float32)
            parts = jnp.einsum('tgh,ghd->tgd', blocks, downs).astype(jnp.bfloat16)
            parts = lax.optimization_barrier(parts).astype(jnp.float32)
            summed = lax.optimization_barrier(jnp.sum(parts, axis=1))
            total = total + jnp.where((chosen == expert)[:, None], summed, jnp.float32(0.0))
        state = (state.astype(jnp.float32) + gate_scale[layer][:, None] * total).astype(jnp.bfloat16)
        results.append(state)
    return jnp.stack(results)
```

```python
import jax
import jax.numpy as jnp
from jax import lax
from jax.experimental import pallas as pl
from jax.experimental.pallas import tpu as pltpu
from jax.sharding import PartitionSpec as P

MESH = pl.DeviceIdType.MESH
EXPERTS = 4
LANES = 128
PARTS = 4
SLOTS = 16
LAG = 2
GRID_Y, GRID_X = 8, 4
PEERS = GRID_Y * GRID_X
SECTIONS = 16
TOK = 6
DX = (2, 1, 3, 0)


def kernel(
    tok_ref, ids_ref, scale_ref, gain_ref, wg_hbm, wu_hbm, wd_hbm, out_ref,
    wgu, wd, tok_stage, tok_recv, meta_send, meta_own, meta_next, meta_init, place_next, place_init,
    disp_send, disp_recv, init_send, part_send, part_recv, res_send, res_init, res_recv, out_send, out_recv,
    w_sem, meta_ss, meta_rs, tok_ss, tok_rs, disp_ss, disp_rs, part_ss, part_rs, res_ss, res_rs, out_ss, out_rs,
):
    s = lax.axis_index("section")
    p = lax.axis_index("expert")
    y, x = p // GRID_X, p % GRID_X
    last = SECTIONS - 1

    loads = [
        pltpu.make_async_copy(wg_hbm.at[0], wgu.at[:, pl.ds(0, LANES)], w_sem.at[0]),
        pltpu.make_async_copy(wu_hbm.at[0], wgu.at[:, pl.ds(LANES, LANES)], w_sem.at[1]),
        pltpu.make_async_copy(wd_hbm.at[0], wd, w_sem.at[2]),
    ]
    for load in loads:
        load.start()

    def everyone(act, skip_self):
        def row(k, _):
            dy = GRID_Y // 2 + ((k + 1) // 2) * (1 - 2 * (k % 2))
            base = ((y + dy) % GRID_Y) * GRID_X
            for dx in DX:
                q = base + (x + dx) % GRID_X
                if skip_self and dx == 0:
                    pl.when(q != p)(lambda q=q: act(q))
                else:
                    act(q)
            return 0

        lax.fori_loop(0, GRID_Y, row, 0)

    def send(src, dst, ss, rs, section, q):
        pltpu.make_async_remote_copy(
            src, dst, ss, rs, device_id=(section, q), device_id_type=MESH
        ).start()

    def drain(ref, sem):
        pltpu.make_async_copy(ref, ref, sem).wait()

    barrier = pltpu.get_barrier_semaphore()

    def greet(section):
        def one(q):
            pl.semaphore_signal(barrier, inc=1, device_id=(section, q), device_id_type=MESH)

        return one

    everyone(greet(s), True)
    pl.when(s > 0)(lambda: everyone(greet(s - 1), False))
    pl.when(s < last)(lambda: everyone(greet(s + 1), False))

    names = [ids_ref[0, t, 0] for t in range(TOK)]
    for t in range(TOK):
        rank = jnp.int32(0)
        for earlier in range(t):
            rank = rank + jnp.where(names[earlier] == names[t], 1, 0)
        slot = names[t] * SLOTS + rank + 2 * (p % 8)
        meta_send[0, pl.ds(t, 1), :] = jnp.full((1, LANES), slot.astype(jnp.float32))
        meta_send[1, pl.ds(t, 1), :] = jnp.full((1, LANES), scale_ref[0, t])
    meta_send[0, pl.ds(TOK, 2), :] = jnp.full((2, LANES), -1.0, jnp.float32)
    meta_send[1, pl.ds(TOK, 2), :] = jnp.zeros((2, LANES), jnp.float32)
    meta_own[p] = meta_send[...]

    @pl.when(s == 1)
    def _():
        for d in range(PEERS):
            tok_stage[d, pl.ds(0, TOK), :] = tok_ref[:, d * LANES:(d + 1) * LANES].astype(jnp.float32)
            tok_stage[d, pl.ds(TOK, 2), :] = jnp.zeros((2, LANES), jnp.float32)
        tok_recv[p] = tok_stage[p]

    met = PEERS - 1 + jnp.where(s > 0, PEERS, 0) + jnp.where(s < last, PEERS, 0)
    pl.semaphore_wait(barrier, met)

    @pl.when(s == 0)
    def _():
        everyone(lambda q: send(meta_send, meta_init.at[p], meta_ss, meta_rs.at[2], 1, q), False)

    @pl.when(s == 1)
    def _():
        everyone(lambda q: send(tok_stage.at[q], tok_recv.at[p], tok_ss, tok_rs, s, q), True)

    everyone(lambda q: send(meta_send, meta_own.at[p], meta_ss, meta_rs.at[0], s, q), True)

    @pl.when(s > 0)
    def _():
        everyone(lambda q: send(meta_send, meta_next.at[p], meta_ss, meta_rs.at[1], s - 1, q), False)

    def places(meta, place):
        for m in range(PARTS):
            slots = meta[8 * m:8 * m + 8, 0].reshape(64, LANES)
            along = jnp.transpose(slots)[:64, :]
            wanted = lax.broadcasted_iota(jnp.int32, (64, 64), 0).astype(jnp.float32)
            place[m] = jnp.where(along == wanted, 1.0, 0.0).astype(jnp.bfloat16)

    def emit(m, rows, place, staged, res, section):
        slotted = jnp.dot(place[m], rows, preferred_element_type=jnp.float32).astype(jnp.bfloat16)
        for e in range(EXPERTS):
            staged[m, e] = slotted[e * SLOTS:(e + 1) * SLOTS]
        everyone(
            lambda q: send(
                staged.at[m, q // 8], disp_recv.at[m, p], disp_ss, disp_rs.at[m], section, q
            ),
            False,
        )
        res[m] = rows
        send(res.at[m], res_recv.at[m], res_ss, res_rs.at[m], section, p)

    @pl.when(s == 1)
    def _():
        drain(meta_init, meta_rs.at[2])
        places(meta_init, place_init)
        drain(tok_recv.at[pl.ds(0, PEERS - 1)], tok_rs)

        def first(m, _):
            rows = tok_recv[pl.ds(8 * m, 8)].reshape(64, LANES).astype(jnp.bfloat16)
            emit(m, rows, place_init, init_send, res_init, 0)
            return 0

        lax.fori_loop(0, PARTS, first, 0)

    drain(meta_own.at[pl.ds(0, PEERS - 1)], meta_rs.at[0])

    @pl.when(s < last)
    def _():
        drain(meta_next, meta_rs.at[1])
        places(meta_next, place_next)

    for load in loads:
        load.wait()

    def work(m):
        drain(disp_recv.at[m], disp_rs.at[m])
        total = jnp.zeros((SLOTS, LANES), jnp.float32)
        acc = jnp.zeros((SLOTS, 2 * LANES), jnp.float32)
        for k in range(0, PEERS, 2):
            pair = []
            for c in (k, k + 1):
                values = disp_recv[m, c].astype(jnp.float32)
                total = total + values * values
                pair.append((values * gain_ref[0:1, c * LANES:(c + 1) * LANES]).astype(jnp.bfloat16))
            acc = acc + jnp.dot(
                jnp.concatenate(pair, axis=1), wgu[k * LANES:(k + 2) * LANES, :],
                preferred_element_type=jnp.float32,
            )
        inverse = lax.rsqrt(jnp.sum(total, axis=1, keepdims=True) * (1.0 / (PEERS * LANES)) + 1e-6)
        gate, upward = acc[:, :LANES] * inverse, acc[:, LANES:] * inverse
        hidden = (gate / (1.0 + jnp.exp(-gate)) * upward).astype(jnp.bfloat16)
        for k in range(0, PEERS, 4):
            part = jnp.dot(
                hidden, wd[:, k * LANES:(k + 4) * LANES], preferred_element_type=jnp.float32
            ).astype(jnp.bfloat16)
            for c in range(4):
                part_send[m, k + c] = part[:, c * LANES:(c + 1) * LANES]
        everyone(
            lambda q: send(part_send.at[m, q], part_recv.at[m, p], part_ss, part_rs.at[m], s, q), True
        )
        part_recv[m, p] = part_send[m, p]

    def own(m):
        drain(res_recv.at[m], res_rs.at[m])
        drain(part_recv.at[m, pl.ds(0, PEERS - 1)], part_rs.at[m])
        summed = []
        for e in range(EXPERTS):
            total = part_recv[m, 8 * e].astype(jnp.float32)
            for g in range(1, 8):
                total = total + part_recv[m, 8 * e + g].astype(jnp.float32)
            summed.append(total)
        summed = jnp.concatenate(summed, axis=0)
        high = summed.astype(jnp.bfloat16)
        low = (summed - high.astype(jnp.float32)).astype(jnp.bfloat16)
        meta = meta_own[pl.ds(8 * m, 8)]
        slots, scales = meta[:, 0].reshape(64, LANES), meta[:, 1].reshape(64, LANES)
        lane = (lax.broadcasted_iota(jnp.int32, (64, LANES), 1) % 64).astype(jnp.float32)
        chosen = jnp.where(slots == lane, 1.0, 0.0).astype(jnp.bfloat16)
        expert_out = jnp.dot(
            chosen, jnp.concatenate([high, low], axis=0), preferred_element_type=jnp.float32
        )
        rows = (res_recv[m].astype(jnp.float32) + scales * expert_out).astype(jnp.bfloat16)
        pl.when(s < last)(lambda: emit(m, rows, place_next, disp_send, res_send, s + 1))
        out_send[m] = rows.astype(jnp.float32).reshape(8, 8, LANES)
        for j in range(8):
            q = 8 * m + j

            @pl.when(q != p)
            def _():
                send(out_send.at[m, j], out_recv.at[p], out_ss, out_rs, s, q)

            @pl.when(q == p)
            def _():
                out_recv[p] = out_send[m, j]

    def step(i, _):
        pl.when(i < PARTS)(lambda: work(i))
        pl.when(i >= LAG)(lambda: own(i - LAG))
        return 0

    lax.fori_loop(0, PARTS + LAG, step, 0)

    drain(out_recv.at[pl.ds(0, PEERS - 1)], out_rs)
    for d in range(PEERS):
        out_ref[0, :, d * LANES:(d + 1) * LANES] = out_recv[d, 0:TOK, :].astype(jnp.bfloat16)

    drain(meta_own.at[pl.ds(0, PEERS - 1)], meta_ss)
    pl.when(s > 0)(lambda: drain(meta_own, meta_ss))
    pl.when(s == 0)(lambda: drain(meta_own, meta_ss))

    @pl.when(s == 1)
    def _():
        drain(tok_recv.at[pl.ds(0, PEERS - 1)], tok_ss)
        drain(disp_recv, disp_ss)
        drain(res_recv, res_ss)

    @pl.when(s < last)
    def _():
        drain(disp_recv, disp_ss)
        drain(res_recv, res_ss)

    drain(part_recv.at[:, pl.ds(0, PEERS - 1)], part_ss)
    drain(out_recv.at[pl.ds(0, PEERS - 1)], out_ss)


def local(tokens, expert_ids, gate_scale, norm_gain, w_gate, w_up, w_down):
    width = tokens.shape[1]
    vmem = pl.BlockSpec(memory_space=pltpu.VMEM)
    smem = pl.BlockSpec(memory_space=pltpu.SMEM)
    hbm = pl.BlockSpec(memory_space=pl.ANY)
    b16, f32 = jnp.bfloat16, jnp.float32
    dma = pltpu.SemaphoreType.DMA
    return pl.pallas_call(
        kernel,
        out_shape=jax.ShapeDtypeStruct((1, TOK, width), b16),
        in_specs=[vmem, smem, smem, vmem, hbm, hbm, hbm],
        out_specs=vmem,
        scratch_shapes=[
            pltpu.VMEM((width, 2 * LANES), b16),
            pltpu.VMEM((LANES, width), b16),
            pltpu.VMEM((PEERS, 8, LANES), f32),
            pltpu.VMEM((PEERS, 8, LANES), f32),
            pltpu.VMEM((2, 8, LANES), f32),
            pltpu.VMEM((PEERS, 2, 8, LANES), f32),
            pltpu.VMEM((PEERS, 2, 8, LANES), f32),
            pltpu.VMEM((PEERS, 2, 8, LANES), f32),
            pltpu.VMEM((PARTS, 64, 64), b16),
            pltpu.VMEM((PARTS, 64, 64), b16),
            pltpu.VMEM((PARTS, EXPERTS, SLOTS, LANES), b16),
            pltpu.VMEM((PARTS, PEERS, SLOTS, LANES), b16),
            pltpu.VMEM((PARTS, EXPERTS, SLOTS, LANES), b16),
            pltpu.VMEM((PARTS, PEERS, SLOTS, LANES), b16),
            pltpu.VMEM((PARTS, PEERS, SLOTS, LANES), b16),
            pltpu.VMEM((PARTS, 64, LANES), b16),
            pltpu.VMEM((PARTS, 64, LANES), b16),
            pltpu.VMEM((PARTS, 64, LANES), b16),
            pltpu.VMEM((PARTS, 8, 8, LANES), f32),
            pltpu.VMEM((PEERS, 8, LANES), f32),
            dma((3,)),
            dma,
            dma((3,)),
            dma,
            dma,
            dma,
            dma((PARTS,)),
            dma,
            dma((PARTS,)),
            dma,
            dma((PARTS,)),
            dma,
            dma,
        ],
        compiler_params=pltpu.CompilerParams(
            collective_id=0, has_side_effects=True, vmem_limit_bytes=32 * 2**20
        ),
    )(tokens, expert_ids, gate_scale, norm_gain, w_gate, w_up, w_down)


def solution(mesh):
    return jax.shard_map(
        local,
        mesh=mesh,
        in_specs=(
            P("expert", None),
            P("section", "expert", None),
            P("section", "expert"),
            P("section", None),
            P("section", None, "expert"),
            P("section", None, "expert"),
            P("section", "expert", None),
        ),
        out_specs=P("section", "expert", None),
        check_vma=False,
    )
```

```python
import jax
import jax.numpy as jnp
from jax import lax
from jax.experimental import pallas as pl
from jax.experimental.pallas import tpu as pltpu
from jax.sharding import PartitionSpec as P

MESH = pl.DeviceIdType.MESH
EXPERTS = 4
LANES = 128
PARTS = 4
SLOTS = 16
LAG = 2
GRID_Y, GRID_X = 8, 4
PEERS = GRID_Y * GRID_X
SECTIONS = 16
TOK = 6
PAIR = 2
EARLY = 2
DX = (2, 1, 3, 0)
FAR_FIRST = (4, 3, 5, 2, 6, 1, 7, 0)
NEAR_FIRST = (0, 1, 7, 2, 6, 3, 5, 4)


def kernel(
    tok_hbm, ids_ref, scale_ref, gain_hbm, wg_hbm, wu_hbm, wd_hbm, out_ref,
    wgu, wd, tok_ref, gain_ref, tok_stage, tok_recv, meta_send, meta_own, meta_next, meta_init, place_next, place_init, chosen, scales,
    disp_send, disp_recv, init_send, part_send, part_recv, res_send, res_init, res_recv, out_send, out_recv, gains, row_sums,
    pair_sums, pair_send, pair_res, pair_out,
    w_sem, move_ss, move_rs, meta_ss, meta_rs, tok_ss, tok_rs, disp_ss, disp_rs, part_ss, part_rs, res_ss, res_rs, out_ss, out_rs,
):
    s = lax.axis_index("section")
    p = lax.axis_index("expert")
    y, x = p // GRID_X, p % GRID_X
    last = SECTIONS - 1

    loads = [
        pltpu.make_async_copy(wg_hbm.at[0], wgu.at[:, pl.ds(0, LANES)], w_sem.at[0]),
        pltpu.make_async_copy(wu_hbm.at[0], wgu.at[:, pl.ds(LANES, LANES)], w_sem.at[1]),
        pltpu.make_async_copy(wd_hbm.at[0], wd.at[pl.ds(0, LANES)], w_sem.at[2]),
    ]
    near = [
        pltpu.make_async_copy(tok_hbm, tok_ref, w_sem.at[3]),
        pltpu.make_async_copy(gain_hbm, gain_ref, w_sem.at[4]),
    ]
    for load in near + loads:
        load.start()

    def row_at(r):
        return (y + r) % GRID_Y

    def in_row(r, act, skip_self):
        base = row_at(r) * GRID_X
        for dx in DX:
            if not (skip_self and r == 0 and dx == 0):
                act(base + (x + dx) % GRID_X, (GRID_Y - r) % GRID_Y)

    def everyone(act, skip_self):
        def one(k, _):
            r = GRID_Y // 2 + ((k + 1) // 2) * (1 - 2 * (k % 2))
            base = ((y + r) % GRID_Y) * GRID_X
            back = (GRID_Y - r) % GRID_Y
            for dx in DX:
                q = base + (x + dx) % GRID_X
                if skip_self and dx == 0:
                    pl.when(q != p)(lambda q=q: act(q, back))
                else:
                    act(q, back)
            return 0

        lax.fori_loop(0, GRID_Y, one, 0)

    def loop(count, body):
        lax.fori_loop(0, count, lambda k, c: (body(k), c)[1], 0)

    def send(src, dst, ss, rs, section, q):
        pltpu.make_async_remote_copy(
            src, dst, ss, rs, device_id=(section, q), device_id_type=MESH
        ).start()

    def drain(ref, sem):
        pltpu.make_async_copy(ref, ref, sem).wait()

    barrier = pltpu.get_barrier_semaphore()

    def greet(section):
        def one(q, r):
            pl.semaphore_signal(barrier, inc=1, device_id=(section, q), device_id_type=MESH)

        return one

    everyone(greet(s), True)
    pl.when(s > 0)(lambda: everyone(greet(s - 1), False))
    pl.when(s < last)(lambda: everyone(greet(s + 1), False))

    names = [ids_ref[0, t] for t in range(TOK)]
    for t in range(TOK):
        rank = jnp.int32(0)
        for earlier in range(t):
            rank = rank + jnp.where(names[earlier] == names[t], 1, 0)
        slot = names[t] * SLOTS + rank + 2 * (p % 8)
        lane = lax.broadcasted_iota(jnp.int32, (1, LANES), 1)
        meta_send[pl.ds(t, 1), :] = jnp.where(lane < 64, slot.astype(jnp.float32), scale_ref[0, t])
    lane = lax.broadcasted_iota(jnp.int32, (2, LANES), 1)
    meta_send[pl.ds(TOK, 2), :] = jnp.where(lane < 64, -1.0, 0.0)
    meta_own[p] = meta_send[...]

    for load in near:
        load.wait()

    @pl.when(s == 1)
    def _():
        def stage(d):
            columns = pl.ds(pl.multiple_of(d * LANES, LANES), LANES)
            tok_stage[d, pl.ds(0, TOK), :] = tok_ref[:, columns].astype(jnp.float32)
            tok_stage[d, pl.ds(TOK, 2), :] = jnp.zeros((2, LANES), jnp.float32)

        loop(PEERS, stage)
        tok_recv[p] = tok_stage[p]

    met = PEERS - 1 + jnp.where(s > 0, PEERS, 0) + jnp.where(s < last, PEERS, 0)
    pl.semaphore_wait(barrier, met)

    @pl.when(s == 0)
    def _():
        everyone(lambda q, r: send(meta_send, meta_init.at[p], meta_ss, meta_rs.at[2], 1, q), False)

    @pl.when(s == 1)
    def _():
        everyone(lambda q, r: send(tok_stage.at[q], tok_recv.at[p], tok_ss, tok_rs, s, q), True)

    late = s >= EARLY
    worker = (x % 2 == 0)

    def moves(q):
        return [
            pltpu.make_async_remote_copy(
                src, dst, move_ss.at[i], move_rs.at[i], device_id=(s, q), device_id_type=MESH
            )
            for i, (src, dst) in enumerate((
                (wg_hbm.at[0], wgu.at[:, pl.ds(2 * LANES, LANES)]),
                (wu_hbm.at[0], wgu.at[:, pl.ds(3 * LANES, LANES)]),
                (wd_hbm.at[0], wd.at[pl.ds(LANES, LANES)]),
            ))
        ]

    @pl.when(late & jnp.logical_not(worker))
    def _():
        aim = jnp.where(s % 2 == 0, x - 1, (x + 1) % GRID_X)
        for move in moves(y * GRID_X + aim):
            move.start()

    def places(meta, place):
        for m in range(PARTS):
            along = jnp.transpose(meta[8 * m:8 * m + 8].reshape(64, LANES))[:64, :]
            wanted = lax.broadcasted_iota(jnp.int32, (64, 64), 0).astype(jnp.float32)
            place[m] = jnp.where(along == wanted, 1.0, 0.0).astype(jnp.bfloat16)

    def emit(m, rows, place, staged, res, section):
        slotted = jnp.dot(place[m], rows, preferred_element_type=jnp.float32).astype(jnp.bfloat16)
        for e in range(EXPERTS):
            staged[m, e] = slotted[e * SLOTS:(e + 1) * SLOTS]
        everyone(
            lambda q, r: pl.when((section < EARLY) | (q % 2 == 0))(
                lambda: send(
                    staged.at[m, q // 8], disp_recv.at[m, p], disp_ss, disp_rs.at[m, r], section, q
                )
            ),
            False,
        )
        res[m] = rows
        early = section < EARLY
        keeper = jnp.where(early, p, y * GRID_X + 2 * (x // 2) + 1)
        send(
            res.at[m], res_recv.at[m, jnp.where(early, 0, x % 2)], res_ss, res_rs.at[m], section, keeper
        )

    @pl.when(s == 1)
    def _():
        drain(meta_init, meta_rs.at[2])
        places(meta_init, place_init)
        drain(tok_recv.at[pl.ds(0, PEERS - 1)], tok_rs)

        def first(m, _):
            rows = tok_recv[pl.ds(8 * m, 8)].reshape(64, LANES).astype(jnp.bfloat16)
            emit(m, rows, place_init, init_send, res_init, 0)
            return 0

        lax.fori_loop(0, PARTS, first, 0)

    everyone(lambda q, r: send(meta_send, meta_own.at[p], meta_ss, meta_rs.at[0], s, q), True)

    @pl.when(s > 0)
    def _():
        everyone(lambda q, r: send(meta_send, meta_next.at[p], meta_ss, meta_rs.at[1], s - 1, q), False)

    drain(meta_own.at[pl.ds(0, PEERS - 1)], meta_rs.at[0])
    for m in range(PARTS):
        rows = meta_own[8 * m:8 * m + 8].reshape(64, LANES)
        lane = (lax.broadcasted_iota(jnp.int32, (64, LANES), 1) % 64).astype(jnp.float32)
        chosen[m] = jnp.where(jnp.broadcast_to(rows[:, 0:1], (64, LANES)) == lane, 1.0, 0.0).astype(jnp.bfloat16)
        scales[m] = jnp.broadcast_to(rows[:, 64:65], (64, LANES))

    @pl.when(s < last)
    def _():
        drain(meta_next, meta_rs.at[1])
        places(meta_next, place_next)

    def spread(d):
        columns = pl.ds(pl.multiple_of(d * LANES, LANES), LANES)
        gains[d] = jnp.broadcast_to(gain_ref[0:1, columns], (SLOTS, LANES))

    loop(PEERS, spread)
    for load in loads:
        load.wait()

    def row_columns(row):
        return pl.ds(pl.multiple_of(row * GRID_X * LANES, GRID_X * LANES), GRID_X * LANES)

    def work(m, blocks):
        total = jnp.zeros((SLOTS, LANES), jnp.float32)
        acc = jnp.zeros((SLOTS, 2 * blocks * LANES), jnp.float32)
        for r in NEAR_FIRST:
            row = row_at(r)
            four = pl.ds(row * GRID_X, GRID_X)
            drain(disp_recv.at[m, four], disp_rs.at[m, r])
            values = disp_recv[m, four].astype(jnp.float32)
            gained = (values * gains[four]).astype(jnp.bfloat16)
            for c in range(GRID_X):
                total = total + values[c] * values[c]
            acc = acc + jnp.dot(
                jnp.concatenate([gained[c] for c in range(GRID_X)], axis=1),
                wgu[row_columns(row), pl.ds(0, 2 * blocks * LANES)],
                preferred_element_type=jnp.float32,
            )
        inverse = lax.rsqrt(jnp.sum(total, axis=1, keepdims=True) * (1.0 / (PEERS * LANES)) + 1e-6)
        hidden = []
        for b in range(blocks):
            gate = acc[:, 2 * b * LANES:(2 * b + 1) * LANES] * inverse
            upward = acc[:, (2 * b + 1) * LANES:(2 * b + 2) * LANES] * inverse
            hidden.append((gate / (1.0 + jnp.exp(-gate)) * upward).astype(jnp.bfloat16))
        hidden = jnp.concatenate(hidden, axis=1)
        for r in FAR_FIRST:
            row = row_at(r)
            part = jnp.dot(
                hidden, wd[pl.ds(0, blocks * LANES), row_columns(row)], preferred_element_type=jnp.float32
            ).astype(jnp.bfloat16)
            for c in range(GRID_X):
                part_send[m, row * GRID_X + c] = part[:, c * LANES:(c + 1) * LANES]
            back = (GRID_Y - r) % GRID_Y
            if blocks == 1:
                in_row(
                    r,
                    lambda q, r: send(
                        part_send.at[m, q], part_recv.at[m, p], part_ss, part_rs.at[m, r], s, q
                    ),
                    True,
                )
            else:
                for j in range(2):
                    send(
                        part_send.at[m, pl.ds(row * GRID_X + 2 * j, PAIR)], part_recv.at[m, pl.ds(p, PAIR)],
                        part_ss, part_rs.at[m, back], s, row * GRID_X + 2 * j + 1,
                    )
        if blocks == 1:
            part_recv[m, p] = part_send[m, p]

    def keep(m):
        for r in NEAR_FIRST:
            row = row_at(r)
            four = pl.ds(row * GRID_X, GRID_X)
            drain(part_recv.at[m, four], part_rs.at[m, r])
            values = part_recv[m, four].astype(jnp.float32)
            pair_sums[row] = values[0:2] + values[2:4]
        summed = []
        for h in range(PAIR):
            summed.append(
                jnp.concatenate([pair_sums[2 * e, h] + pair_sums[2 * e + 1, h] for e in range(EXPERTS)], axis=0)
            )
        summed = jnp.concatenate(summed, axis=1)
        high = summed.astype(jnp.bfloat16)
        low = (summed - high.astype(jnp.float32)).astype(jnp.bfloat16)
        expert_out = jnp.dot(
            chosen[m], jnp.concatenate([high, low], axis=0), preferred_element_type=jnp.float32
        )
        drain(res_recv.at[m], res_rs.at[m])
        before = jnp.concatenate([res_recv[m, h] for h in range(PAIR)], axis=1).astype(jnp.float32)
        scale = jnp.concatenate([scales[m]] * PAIR, axis=1)
        rows = (before + scale * expert_out).astype(jnp.bfloat16)

        @pl.when(s < last)
        def _():
            slotted = jnp.dot(place_next[m], rows, preferred_element_type=jnp.float32).astype(jnp.bfloat16)
            for e in range(EXPERTS):
                for h in range(PAIR):
                    pair_send[m, e, h] = slotted[e * SLOTS:(e + 1) * SLOTS, h * LANES:(h + 1) * LANES]
            for r in FAR_FIRST:
                row = row_at(r)
                for j in range(2):
                    send(
                        pair_send.at[m, row // 2], disp_recv.at[m, pl.ds(p - 1, PAIR)],
                        disp_ss, disp_rs.at[m, (GRID_Y - r) % GRID_Y], s + 1, row * GRID_X + 2 * j,
                    )
            for h in range(PAIR):
                pair_res[m, h] = rows[:, h * LANES:(h + 1) * LANES]
            send(pair_res.at[m], res_recv.at[m], res_ss, res_rs.at[m], s + 1, p)

        shown = rows.astype(jnp.float32)
        for h in range(PAIR):
            pair_out[m, :, h] = shown[:, h * LANES:(h + 1) * LANES].reshape(8, 8, LANES)
        pl.when(s == last)(lambda: deliver_pair(m))

    def deliver_pair(m):
        mine = pl.ds(p - 1, PAIR)

        def one(j):
            q = 8 * m + j
            pl.when(q != p)(lambda: send(pair_out.at[m, j], out_recv.at[mine], out_ss, out_rs, s, q))

            @pl.when(q == p)
            def _():
                out_recv[mine] = pair_out[m, j]

        loop(8, one)

    def deliver(m):
        for j in range(8):
            q = 8 * m + j

            @pl.when(q != p)
            def _():
                send(out_send.at[m, j], out_recv.at[p], out_ss, out_rs, s, q)

            @pl.when(q == p)
            def _():
                out_recv[p] = out_send[m, j]

    def own(m):
        drain(res_recv.at[m, 0], res_rs.at[m])
        for r in NEAR_FIRST:
            row = row_at(r)
            count = GRID_X - 1 if r == 0 else GRID_X
            drain(part_recv.at[m, pl.ds(row * GRID_X, count)], part_rs.at[m, r])
            four = part_recv[m, pl.ds(row * GRID_X, GRID_X)].astype(jnp.float32)
            row_sums[row] = (four[0] + four[1]) + (four[2] + four[3])
        summed = [row_sums[2 * e] + row_sums[2 * e + 1] for e in range(EXPERTS)]
        summed = jnp.concatenate(summed, axis=0)
        high = summed.astype(jnp.bfloat16)
        low = (summed - high.astype(jnp.float32)).astype(jnp.bfloat16)
        expert_out = jnp.dot(
            chosen[m], jnp.concatenate([high, low], axis=0), preferred_element_type=jnp.float32
        )
        rows = (res_recv[m, 0].astype(jnp.float32) + scales[m] * expert_out).astype(jnp.bfloat16)
        pl.when(s < last)(lambda: emit(m, rows, place_next, disp_send, res_send, s + 1))
        out_send[m] = rows.astype(jnp.float32).reshape(8, 8, LANES)
    @pl.when(s < EARLY)
    def _():
        def step(i):
            pl.when(i < PARTS)(lambda: work(i, 1))
            pl.when(i >= LAG)(lambda: own(i - LAG))

        loop(PARTS + LAG, step)
        loop(PARTS, deliver)

    @pl.when(late & worker)
    def _():
        for move in moves(p):
            move.wait_recv()
        loop(PARTS, lambda m: work(m, 2))

    @pl.when(late & jnp.logical_not(worker))
    def _():
        loop(PARTS, keep)

        @pl.when(s < last)
        def _():
            loop(PARTS, deliver_pair)

        for move in moves(p):
            move.wait_send()

    pl.when(s < EARLY)(lambda: drain(out_recv.at[pl.ds(0, PEERS - 1)], out_rs))
    pl.when(late & worker)(lambda: drain(out_recv, out_rs))
    pl.when(late & jnp.logical_not(worker))(lambda: drain(out_recv.at[pl.ds(0, PEERS - PAIR)], out_rs))

    def store(d):
        columns = pl.ds(pl.multiple_of(d * LANES, LANES), LANES)
        out_ref[0, :, columns] = out_recv[d, 0:TOK, :].astype(jnp.bfloat16)

    loop(PEERS, store)

    drain(meta_own.at[pl.ds(0, PEERS - 1)], meta_ss)
    pl.when(s > 0)(lambda: drain(meta_own, meta_ss))
    pl.when(s == 0)(lambda: drain(meta_own, meta_ss))

    half = PEERS // 2

    @pl.when(s == 0)
    def _():
        drain(disp_recv, disp_ss)
        drain(res_recv.at[:, 0], res_ss)

    @pl.when(s == 1)
    def _():
        drain(tok_recv.at[pl.ds(0, PEERS - 1)], tok_ss)
        drain(disp_recv, disp_ss)
        drain(disp_recv.at[:, pl.ds(0, half)], disp_ss)
        drain(res_recv, res_ss)

    @pl.when(s < EARLY)
    def _():
        drain(part_recv.at[:, pl.ds(0, PEERS - 1)], part_ss)
        drain(out_recv.at[pl.ds(0, PEERS - 1)], out_ss)

    pl.when(late & worker)(lambda: drain(part_recv, part_ss))

    @pl.when(late & jnp.logical_not(worker))
    def _():
        drain(out_recv, out_ss)
        drain(out_recv.at[pl.ds(0, PEERS - PAIR)], out_ss)

        @pl.when(s < last)
        def _():
            drain(disp_recv, disp_ss)
            drain(res_recv, res_ss)


def local(tokens, expert_ids, gate_scale, norm_gain, w_gate, w_up, w_down):
    width = tokens.shape[1]
    vmem = pl.BlockSpec(memory_space=pltpu.VMEM)
    smem = pl.BlockSpec(memory_space=pltpu.SMEM)
    hbm = pl.BlockSpec(memory_space=pltpu.HBM)
    b16, f32 = jnp.bfloat16, jnp.float32
    dma = pltpu.SemaphoreType.DMA
    return pl.pallas_call(
        kernel,
        out_shape=jax.ShapeDtypeStruct((1, TOK, width), b16),
        in_specs=[hbm, smem, smem, hbm, hbm, hbm, hbm],
        out_specs=vmem,
        scratch_shapes=[
            pltpu.VMEM((width, 4 * LANES), b16),
            pltpu.VMEM((2 * LANES, width), b16),
            pltpu.VMEM((TOK, width), b16),
            pltpu.VMEM((1, width), f32),
            pltpu.VMEM((PEERS, 8, LANES), f32),
            pltpu.VMEM((PEERS, 8, LANES), f32),
            pltpu.VMEM((8, LANES), f32),
            pltpu.VMEM((PEERS, 8, LANES), f32),
            pltpu.VMEM((PEERS, 8, LANES), f32),
            pltpu.VMEM((PEERS, 8, LANES), f32),
            pltpu.VMEM((PARTS, 64, 64), b16),
            pltpu.VMEM((PARTS, 64, 64), b16),
            pltpu.VMEM((PARTS, 64, LANES), b16),
            pltpu.VMEM((PARTS, 64, LANES), f32),
            pltpu.VMEM((PARTS, EXPERTS, SLOTS, LANES), b16),
            pltpu.VMEM((PARTS, PEERS, SLOTS, LANES), b16),
            pltpu.VMEM((PARTS, EXPERTS, SLOTS, LANES), b16),
            pltpu.VMEM((PARTS, PEERS, SLOTS, LANES), b16),
            pltpu.VMEM((PARTS, PEERS, SLOTS, LANES), b16),
            pltpu.VMEM((PARTS, 64, LANES), b16),
            pltpu.VMEM((PARTS, 64, LANES), b16),
            pltpu.VMEM((PARTS, PAIR, 64, LANES), b16),
            pltpu.VMEM((PARTS, 8, 8, LANES), f32),
            pltpu.VMEM((PEERS, 8, LANES), f32),
            pltpu.VMEM((PEERS, SLOTS, LANES), f32),
            pltpu.VMEM((GRID_Y, SLOTS, LANES), f32),
            pltpu.VMEM((GRID_Y, PAIR, SLOTS, LANES), f32),
            pltpu.VMEM((PARTS, EXPERTS, PAIR, SLOTS, LANES), b16),
            pltpu.VMEM((PARTS, PAIR, 64, LANES), b16),
            pltpu.VMEM((PARTS, 8, PAIR, 8, LANES), f32),
            dma((5,)),
            dma((3,)),
            dma((3,)),
            dma,
            dma((3,)),
            dma,
            dma,
            dma,
            dma((PARTS, GRID_Y)),
            dma,
            dma((PARTS, GRID_Y)),
            dma,
            dma((PARTS,)),
            dma,
            dma,
        ],
        compiler_params=pltpu.CompilerParams(
            collective_id=0, has_side_effects=True, vmem_limit_bytes=60 * 2**20
        ),
    )(tokens, expert_ids[:, :, 0], gate_scale, norm_gain, w_gate, w_up, w_down)


def solution(mesh):
    return jax.shard_map(
        local,
        mesh=mesh,
        in_specs=(
            P("expert", None),
            P("section", "expert", None),
            P("section", "expert"),
            P("section", None),
            P("section", None, "expert"),
            P("section", None, "expert"),
            P("section", "expert", None),
        ),
        out_specs=P("section", "expert", None),
        check_vma=False,
    )
```

```python
import jax
import jax.numpy as jnp
from jax import lax
from jax.experimental import pallas as pl
from jax.experimental.pallas import tpu as pltpu
from jax.sharding import PartitionSpec as P

MESH = pl.DeviceIdType.MESH
EXPERTS = 4
LANES = 128
PARTS = 4
SLOTS = 16
LAG = 2
GRID_Y, GRID_X = 8, 4
PEERS = GRID_Y * GRID_X
SECTIONS = 16
TOK = 6
PAIR = 2
EARLY = 2
DX = (2, 1, 3, 0)
FAR_FIRST = (4, 3, 5, 2, 6, 1, 7, 0)
ARRIVALS = ((0, 1, 7), (2, 6), (3, 5), (4,))
LEAVING = ((4,), (3, 5, 2, 6), (1, 7, 0))
NEAR_FIRST = (0, 1, 7, 2, 6, 3, 5, 4)


def kernel(
    tok_hbm, ids_ref, scale_ref, gain_hbm, wg_hbm, wu_hbm, wd_hbm, out_ref,
    wgu, wd, tok_ref, gain_ref, tok_stage, tok_recv, meta_send, meta_own, meta_next, meta_init, place_next, place_init, chosen, scales,
    disp_send, disp_recv, init_send, part_send, part_recv, res_send, res_init, res_recv, out_send, out_recv, gains, row_sums,
    pair_sums, pair_send, pair_res, pair_out, hop, hop_scale, placed,
    w_sem, move_ss, move_rs, meta_ss, meta_rs, tok_ss, tok_rs, disp_ss, disp_rs, part_ss, part_rs, res_ss, res_rs, out_ss, out_rs,
):
    s = lax.axis_index("section")
    p = lax.axis_index("expert")
    y, x = p // GRID_X, p % GRID_X
    last = SECTIONS - 1

    loads = [
        pltpu.make_async_copy(wg_hbm.at[0], wgu.at[:, pl.ds(0, LANES)], w_sem.at[0]),
        pltpu.make_async_copy(wu_hbm.at[0], wgu.at[:, pl.ds(LANES, LANES)], w_sem.at[1]),
        pltpu.make_async_copy(wd_hbm.at[0], wd.at[pl.ds(0, LANES)], w_sem.at[2]),
    ]
    near = [
        pltpu.make_async_copy(tok_hbm, tok_ref, w_sem.at[3]),
        pltpu.make_async_copy(gain_hbm, gain_ref, w_sem.at[4]),
    ]
    for load in near + loads:
        load.start()

    def row_at(r):
        return (y + r) % GRID_Y

    def in_row(r, act, skip_self):
        base = row_at(r) * GRID_X
        for dx in DX:
            if not (skip_self and r == 0 and dx == 0):
                act(base + (x + dx) % GRID_X, (GRID_Y - r) % GRID_Y)

    def everyone(act, skip_self):
        def one(k, _):
            r = GRID_Y // 2 + ((k + 1) // 2) * (1 - 2 * (k % 2))
            base = ((y + r) % GRID_Y) * GRID_X
            back = (GRID_Y - r) % GRID_Y
            for dx in DX:
                q = base + (x + dx) % GRID_X
                if skip_self and dx == 0:
                    pl.when(q != p)(lambda q=q: act(q, back))
                else:
                    act(q, back)
            return 0

        lax.fori_loop(0, GRID_Y, one, 0)

    def loop(count, body):
        lax.fori_loop(0, count, lambda k, c: (body(k), c)[1], 0)

    def send(src, dst, ss, rs, section, q):
        pltpu.make_async_remote_copy(
            src, dst, ss, rs, device_id=(section, q), device_id_type=MESH
        ).start()

    def drain(ref, sem):
        pltpu.make_async_copy(ref, ref, sem).wait()

    barrier = pltpu.get_barrier_semaphore()

    def greet(section):
        def one(q, r):
            pl.semaphore_signal(barrier, inc=1, device_id=(section, q), device_id_type=MESH)

        return one

    everyone(greet(s), True)
    pl.when(s > 0)(lambda: everyone(greet(s - 1), False))
    pl.when(s < last)(lambda: everyone(greet(s + 1), False))

    names = [ids_ref[0, t] for t in range(TOK)]
    for t in range(TOK):
        rank = jnp.int32(0)
        for earlier in range(t):
            rank = rank + jnp.where(names[earlier] == names[t], 1, 0)
        slot = names[t] * SLOTS + rank + 2 * (p % 8)
        lane = lax.broadcasted_iota(jnp.int32, (1, LANES), 1)
        meta_send[pl.ds(t, 1), :] = jnp.where(lane < 64, slot.astype(jnp.float32), scale_ref[0, t])
    lane = lax.broadcasted_iota(jnp.int32, (2, LANES), 1)
    meta_send[pl.ds(TOK, 2), :] = jnp.where(lane < 64, -1.0, 0.0)
    meta_own[p] = meta_send[...]

    for load in near:
        load.wait()

    @pl.when(s == 1)
    def _():
        def stage(d):
            columns = pl.ds(pl.multiple_of(d * LANES, LANES), LANES)
            tok_stage[d, pl.ds(0, TOK), :] = tok_ref[:, columns].astype(jnp.float32)
            tok_stage[d, pl.ds(TOK, 2), :] = jnp.zeros((2, LANES), jnp.float32)

        loop(PEERS, stage)
        tok_recv[p] = tok_stage[p]

    met = PEERS - 1 + jnp.where(s > 0, PEERS, 0) + jnp.where(s < last, PEERS, 0)
    pl.semaphore_wait(barrier, met)

    @pl.when(s == 0)
    def _():
        everyone(lambda q, r: send(meta_send, meta_init.at[p], meta_ss, meta_rs.at[2], 1, q), False)

    @pl.when(s == 1)
    def _():
        everyone(lambda q, r: send(tok_stage.at[q], tok_recv.at[p], tok_ss, tok_rs, s, q), True)

    late = s >= EARLY
    worker = (x % 2 == 0)

    def moves(q):
        return [
            pltpu.make_async_remote_copy(
                src, dst, move_ss.at[i], move_rs.at[i], device_id=(s, q), device_id_type=MESH
            )
            for i, (src, dst) in enumerate((
                (wg_hbm.at[0], wgu.at[:, pl.ds(2 * LANES, LANES)]),
                (wu_hbm.at[0], wgu.at[:, pl.ds(3 * LANES, LANES)]),
                (wd_hbm.at[0], wd.at[pl.ds(LANES, LANES)]),
            ))
        ]

    @pl.when(late & jnp.logical_not(worker))
    def _():
        aim = jnp.where(s % 2 == 0, x - 1, (x + 1) % GRID_X)
        for move in moves(y * GRID_X + aim):
            move.start()

    def places(meta, place):
        for m in range(PARTS):
            along = jnp.transpose(meta[8 * m:8 * m + 8].reshape(64, LANES))[:64, :]
            wanted = lax.broadcasted_iota(jnp.int32, (64, 64), 0).astype(jnp.float32)
            place[m] = jnp.where(along == wanted, 1.0, 0.0).astype(jnp.bfloat16)

    def emit(m, rows, place, staged, res, section):
        slotted = jnp.dot(place[m], rows, preferred_element_type=jnp.float32).astype(jnp.bfloat16)
        for e in range(EXPERTS):
            staged[m, e] = slotted[e * SLOTS:(e + 1) * SLOTS]
        everyone(
            lambda q, r: pl.when((section < EARLY) | (q % 2 == 0))(
                lambda: send(
                    staged.at[m, q // 8], disp_recv.at[m, p], disp_ss, disp_rs.at[m, r], section, q
                )
            ),
            False,
        )
        res[m] = rows
        early = section < EARLY
        keeper = jnp.where(early, p, y * GRID_X + 2 * (x // 2) + 1)
        send(
            res.at[m], res_recv.at[m, jnp.where(early, 0, x % 2)], res_ss, res_rs.at[m], section, keeper
        )

    @pl.when(s == 1)
    def _():
        drain(meta_init, meta_rs.at[2])
        places(meta_init, place_init)
        drain(tok_recv.at[pl.ds(0, PEERS - 1)], tok_rs)

        def first(m, _):
            rows = tok_recv[pl.ds(8 * m, 8)].reshape(64, LANES).astype(jnp.bfloat16)
            emit(m, rows, place_init, init_send, res_init, 0)
            return 0

        lax.fori_loop(0, PARTS, first, 0)

    everyone(lambda q, r: send(meta_send, meta_own.at[p], meta_ss, meta_rs.at[0], s, q), True)

    @pl.when(s > 0)
    def _():
        everyone(lambda q, r: send(meta_send, meta_next.at[p], meta_ss, meta_rs.at[1], s - 1, q), False)

    drain(meta_own.at[pl.ds(0, PEERS - 1)], meta_rs.at[0])
    for m in range(PARTS):
        rows = meta_own[8 * m:8 * m + 8].reshape(64, LANES)
        lane = (lax.broadcasted_iota(jnp.int32, (64, LANES), 1) % 64).astype(jnp.float32)
        chosen[m] = jnp.where(jnp.broadcast_to(rows[:, 0:1], (64, LANES)) == lane, 1.0, 0.0).astype(jnp.bfloat16)
        scales[m] = jnp.broadcast_to(rows[:, 64:65], (64, LANES))

    @pl.when(s < last)
    def _():
        drain(meta_next, meta_rs.at[1])
        places(meta_next, place_next)

        def join(m):
            hop[m] = jnp.dot(place_next[m], chosen[m], preferred_element_type=jnp.float32).astype(jnp.bfloat16)
            hop_scale[m] = jnp.dot(
                place_next[m].astype(jnp.float32), scales[m],
                preferred_element_type=jnp.float32, precision=lax.Precision.HIGHEST,
            )

        loop(PARTS, join)

    def spread(d):
        columns = pl.ds(pl.multiple_of(d * LANES, LANES), LANES)
        gains[d] = jnp.broadcast_to(gain_ref[0:1, columns], (SLOTS, LANES))

    loop(PEERS, spread)
    for load in loads:
        load.wait()

    def row_columns(row):
        return pl.ds(pl.multiple_of(row * GRID_X * LANES, GRID_X * LANES), GRID_X * LANES)

    def work(m, blocks):
        total = jnp.zeros((SLOTS, LANES), jnp.float32)
        acc = jnp.zeros((SLOTS, 2 * blocks * LANES), jnp.float32)
        for group in ARRIVALS:
            for r in group:
                drain(disp_recv.at[m, pl.ds(row_at(r) * GRID_X, GRID_X)], disp_rs.at[m, r])
            for r in group:
                row = row_at(r)
                four = pl.ds(row * GRID_X, GRID_X)
                values = disp_recv[m, four].astype(jnp.float32)
                gained = (values * gains[four]).astype(jnp.bfloat16)
                for c in range(GRID_X):
                    total = total + values[c] * values[c]
                acc = acc + jnp.dot(
                    jnp.concatenate([gained[c] for c in range(GRID_X)], axis=1),
                    wgu[row_columns(row), pl.ds(0, 2 * blocks * LANES)],
                    preferred_element_type=jnp.float32,
                )
        inverse = lax.rsqrt(jnp.sum(total, axis=1, keepdims=True) * (1.0 / (PEERS * LANES)) + 1e-6)
        hidden = []
        for b in range(blocks):
            gate = acc[:, 2 * b * LANES:(2 * b + 1) * LANES] * inverse
            upward = acc[:, (2 * b + 1) * LANES:(2 * b + 2) * LANES] * inverse
            hidden.append((gate / (1.0 + jnp.exp(-gate)) * upward).astype(jnp.bfloat16))
        hidden = jnp.concatenate(hidden, axis=1)
        for group in LEAVING:
            for r in group:
                row = row_at(r)
                part = jnp.dot(
                    hidden, wd[pl.ds(0, blocks * LANES), row_columns(row)], preferred_element_type=jnp.float32
                ).astype(jnp.bfloat16)
                for c in range(GRID_X):
                    part_send[m, row * GRID_X + c] = part[:, c * LANES:(c + 1) * LANES]
            for r in group:
                if blocks == 1:
                    in_row(
                        r,
                        lambda q, r: send(
                            part_send.at[m, q], part_recv.at[m, p], part_ss, part_rs.at[m, r], s, q
                        ),
                        True,
                    )
                else:
                    row = row_at(r)
                    for j in range(2):
                        send(
                            part_send.at[m, pl.ds(row * GRID_X + 2 * j, PAIR)], part_recv.at[m, pl.ds(p, PAIR)],
                            part_ss, part_rs.at[m, (GRID_Y - r) % GRID_Y], s, row * GRID_X + 2 * j + 1,
                        )
        if blocks == 1:
            part_recv[m, p] = part_send[m, p]

    def keep(m):
        drain(res_recv.at[m], res_rs.at[m])

        @pl.when(s < last)
        def _():
            for h in range(PAIR):
                placed[h] = jnp.dot(place_next[m], res_recv[m, h], preferred_element_type=jnp.float32)

        for group in ARRIVALS:
            for r in group:
                drain(part_recv.at[m, pl.ds(row_at(r) * GRID_X, GRID_X)], part_rs.at[m, r])
            for r in group:
                row = row_at(r)
                values = part_recv[m, pl.ds(row * GRID_X, GRID_X)].astype(jnp.float32)
                pair_sums[row] = values[0:2] + values[2:4]
        summed = []
        for h in range(PAIR):
            summed.append(
                jnp.concatenate([pair_sums[2 * e, h] + pair_sums[2 * e + 1, h] for e in range(EXPERTS)], axis=0)
            )
        summed = jnp.concatenate(summed, axis=1)
        high = summed.astype(jnp.bfloat16)
        low = (summed - high.astype(jnp.float32)).astype(jnp.bfloat16)
        both = jnp.concatenate([high, low], axis=0)

        @pl.when(s < last)
        def _():
            moved = jnp.dot(hop[m], both, preferred_element_type=jnp.float32)
            for h in range(PAIR):
                slotted = placed[h] + hop_scale[m] * moved[:, h * LANES:(h + 1) * LANES]
                slotted = slotted.astype(jnp.bfloat16)
                for e in range(EXPERTS):
                    pair_send[m, e, h] = slotted[e * SLOTS:(e + 1) * SLOTS]
            for r in FAR_FIRST:
                row = row_at(r)
                for j in range(2):
                    send(
                        pair_send.at[m, row // 2], disp_recv.at[m, pl.ds(p - 1, PAIR)],
                        disp_ss, disp_rs.at[m, (GRID_Y - r) % GRID_Y], s + 1, row * GRID_X + 2 * j,
                    )

        expert_out = jnp.dot(chosen[m], both, preferred_element_type=jnp.float32)
        before = jnp.concatenate([res_recv[m, h] for h in range(PAIR)], axis=1).astype(jnp.float32)
        scale = jnp.concatenate([scales[m]] * PAIR, axis=1)
        rows = (before + scale * expert_out).astype(jnp.bfloat16)

        @pl.when(s < last)
        def _():
            for h in range(PAIR):
                pair_res[m, h] = rows[:, h * LANES:(h + 1) * LANES]
            send(pair_res.at[m], res_recv.at[m], res_ss, res_rs.at[m], s + 1, p)

        shown = rows.astype(jnp.float32)
        for h in range(PAIR):
            pair_out[m, :, h] = shown[:, h * LANES:(h + 1) * LANES].reshape(8, 8, LANES)
        pl.when(s == last)(lambda: deliver_pair(m))

    def deliver_pair(m):
        mine = pl.ds(p - 1, PAIR)

        def one(j):
            q = 8 * m + j
            pl.when(q != p)(lambda: send(pair_out.at[m, j], out_recv.at[mine], out_ss, out_rs, s, q))

            @pl.when(q == p)
            def _():
                out_recv[mine] = pair_out[m, j]

        loop(8, one)

    def deliver(m):
        for j in range(8):
            q = 8 * m + j

            @pl.when(q != p)
            def _():
                send(out_send.at[m, j], out_recv.at[p], out_ss, out_rs, s, q)

            @pl.when(q == p)
            def _():
                out_recv[p] = out_send[m, j]

    def own(m):
        drain(res_recv.at[m, 0], res_rs.at[m])
        for r in NEAR_FIRST:
            row = row_at(r)
            count = GRID_X - 1 if r == 0 else GRID_X
            drain(part_recv.at[m, pl.ds(row * GRID_X, count)], part_rs.at[m, r])
            four = part_recv[m, pl.ds(row * GRID_X, GRID_X)].astype(jnp.float32)
            row_sums[row] = (four[0] + four[1]) + (four[2] + four[3])
        summed = [row_sums[2 * e] + row_sums[2 * e + 1] for e in range(EXPERTS)]
        summed = jnp.concatenate(summed, axis=0)
        high = summed.astype(jnp.bfloat16)
        low = (summed - high.astype(jnp.float32)).astype(jnp.bfloat16)
        expert_out = jnp.dot(
            chosen[m], jnp.concatenate([high, low], axis=0), preferred_element_type=jnp.float32
        )
        rows = (res_recv[m, 0].astype(jnp.float32) + scales[m] * expert_out).astype(jnp.bfloat16)
        pl.when(s < last)(lambda: emit(m, rows, place_next, disp_send, res_send, s + 1))
        out_send[m] = rows.astype(jnp.float32).reshape(8, 8, LANES)
    @pl.when(s < EARLY)
    def _():
        def step(i):
            pl.when(i < PARTS)(lambda: work(i, 1))
            pl.when(i >= LAG)(lambda: own(i - LAG))

        loop(PARTS + LAG, step)
        loop(PARTS, deliver)

    @pl.when(late & worker)
    def _():
        for move in moves(p):
            move.wait_recv()
        loop(PARTS, lambda m: work(m, 2))

    @pl.when(late & jnp.logical_not(worker))
    def _():
        loop(PARTS, keep)

        @pl.when(s < last)
        def _():
            loop(PARTS, deliver_pair)

        for move in moves(p):
            move.wait_send()

    pl.when(s < EARLY)(lambda: drain(out_recv.at[pl.ds(0, PEERS - 1)], out_rs))
    pl.when(late & worker)(lambda: drain(out_recv, out_rs))
    pl.when(late & jnp.logical_not(worker))(lambda: drain(out_recv.at[pl.ds(0, PEERS - PAIR)], out_rs))

    def store(d):
        columns = pl.ds(pl.multiple_of(d * LANES, LANES), LANES)
        out_ref[0, :, columns] = out_recv[d, 0:TOK, :].astype(jnp.bfloat16)

    loop(PEERS, store)

    drain(meta_own.at[pl.ds(0, PEERS - 1)], meta_ss)
    pl.when(s > 0)(lambda: drain(meta_own, meta_ss))
    pl.when(s == 0)(lambda: drain(meta_own, meta_ss))

    half = PEERS // 2

    @pl.when(s == 0)
    def _():
        drain(disp_recv, disp_ss)
        drain(res_recv.at[:, 0], res_ss)

    @pl.when(s == 1)
    def _():
        drain(tok_recv.at[pl.ds(0, PEERS - 1)], tok_ss)
        drain(disp_recv, disp_ss)
        drain(disp_recv.at[:, pl.ds(0, half)], disp_ss)
        drain(res_recv, res_ss)

    @pl.when(s < EARLY)
    def _():
        drain(part_recv.at[:, pl.ds(0, PEERS - 1)], part_ss)
        drain(out_recv.at[pl.ds(0, PEERS - 1)], out_ss)

    pl.when(late & worker)(lambda: drain(part_recv, part_ss))

    @pl.when(late & jnp.logical_not(worker))
    def _():
        drain(out_recv, out_ss)
        drain(out_recv.at[pl.ds(0, PEERS - PAIR)], out_ss)

        @pl.when(s < last)
        def _():
            drain(disp_recv, disp_ss)
            drain(res_recv, res_ss)


def local(tokens, expert_ids, gate_scale, norm_gain, w_gate, w_up, w_down):
    width = tokens.shape[1]
    vmem = pl.BlockSpec(memory_space=pltpu.VMEM)
    smem = pl.BlockSpec(memory_space=pltpu.SMEM)
    hbm = pl.BlockSpec(memory_space=pltpu.HBM)
    b16, f32 = jnp.bfloat16, jnp.float32
    dma = pltpu.SemaphoreType.DMA
    return pl.pallas_call(
        kernel,
        out_shape=jax.ShapeDtypeStruct((1, TOK, width), b16),
        in_specs=[hbm, smem, smem, hbm, hbm, hbm, hbm],
        out_specs=vmem,
        scratch_shapes=[
            pltpu.VMEM((width, 4 * LANES), b16),
            pltpu.VMEM((2 * LANES, width), b16),
            pltpu.VMEM((TOK, width), b16),
            pltpu.VMEM((1, width), f32),
            pltpu.VMEM((PEERS, 8, LANES), f32),
            pltpu.VMEM((PEERS, 8, LANES), f32),
            pltpu.VMEM((8, LANES), f32),
            pltpu.VMEM((PEERS, 8, LANES), f32),
            pltpu.VMEM((PEERS, 8, LANES), f32),
            pltpu.VMEM((PEERS, 8, LANES), f32),
            pltpu.VMEM((PARTS, 64, 64), b16),
            pltpu.VMEM((PARTS, 64, 64), b16),
            pltpu.VMEM((PARTS, 64, LANES), b16),
            pltpu.VMEM((PARTS, 64, LANES), f32),
            pltpu.VMEM((PARTS, EXPERTS, SLOTS, LANES), b16),
            pltpu.VMEM((PARTS, PEERS, SLOTS, LANES), b16),
            pltpu.VMEM((PARTS, EXPERTS, SLOTS, LANES), b16),
            pltpu.VMEM((PARTS, PEERS, SLOTS, LANES), b16),
            pltpu.VMEM((PARTS, PEERS, SLOTS, LANES), b16),
            pltpu.VMEM((PARTS, 64, LANES), b16),
            pltpu.VMEM((PARTS, 64, LANES), b16),
            pltpu.VMEM((PARTS, PAIR, 64, LANES), b16),
            pltpu.VMEM((PARTS, 8, 8, LANES), f32),
            pltpu.VMEM((PEERS, 8, LANES), f32),
            pltpu.VMEM((PEERS, SLOTS, LANES), f32),
            pltpu.VMEM((GRID_Y, SLOTS, LANES), f32),
            pltpu.VMEM((GRID_Y, PAIR, SLOTS, LANES), f32),
            pltpu.VMEM((PARTS, EXPERTS, PAIR, SLOTS, LANES), b16),
            pltpu.VMEM((PARTS, PAIR, 64, LANES), b16),
            pltpu.VMEM((PARTS, 8, PAIR, 8, LANES), f32),
            pltpu.VMEM((PARTS, 64, LANES), b16),
            pltpu.VMEM((PARTS, 64, LANES), f32),
            pltpu.VMEM((PAIR, 64, LANES), f32),
            dma((5,)),
            dma((3,)),
            dma((3,)),
            dma,
            dma((3,)),
            dma,
            dma,
            dma,
            dma((PARTS, GRID_Y)),
            dma,
            dma((PARTS, GRID_Y)),
            dma,
            dma((PARTS,)),
            dma,
            dma,
        ],
        compiler_params=pltpu.CompilerParams(
            collective_id=0, has_side_effects=True, vmem_limit_bytes=60 * 2**20
        ),
    )(tokens, expert_ids[:, :, 0], gate_scale, norm_gain, w_gate, w_up, w_down)


def solution(mesh):
    return jax.shard_map(
        local,
        mesh=mesh,
        in_specs=(
            P("expert", None),
            P("section", "expert", None),
            P("section", "expert"),
            P("section", None),
            P("section", None, "expert"),
            P("section", None, "expert"),
            P("section", "expert", None),
        ),
        out_specs=P("section", "expert", None),
        check_vma=False,
    )
```

```python
import jax
import jax.numpy as jnp
from jax import lax
from jax.experimental import pallas as pl
from jax.experimental.pallas import tpu as pltpu
from jax.sharding import PartitionSpec as P

MESH = pl.DeviceIdType.MESH
EXPERTS = 4
LANES = 128
PARTS = 4
SLOTS = 16
LAG = 2
GRID_Y, GRID_X = 8, 4
PEERS = GRID_Y * GRID_X
SECTIONS = 16
TOK = 6
PAIR = 2
EARLY = 2
DX = (2, 1, 3, 0)
FAR_FIRST = (4, 3, 5, 2, 6, 1, 7, 0)
ARRIVALS = ((0, 1, 7), (2, 6), (3, 5), (4,))
LEAVING = ((4,), (3, 5, 2, 6), (1, 7, 0))
NEAR_FIRST = (0, 1, 7, 2, 6, 3, 5, 4)


def kernel(
    tok_hbm, ids_ref, scale_ref, gain_hbm, wg_hbm, wu_hbm, wd_hbm, out_ref,
    wgu, wd, tok_ref, gain_ref, tok_stage, tok_recv, meta_send, meta_own, meta_next, meta_init, place_next, place_init, chosen, scales,
    disp_send, disp_recv, init_send, part_send, part_recv, res_send, res_init, res_recv, out_send, out_recv, gains, row_sums,
    pair_sums, pair_send, pair_res, pair_out, hop, hop_scale, placed,
    w_sem, move_ss, move_rs, meta_ss, meta_rs, tok_ss, tok_rs, disp_ss, disp_rs, part_ss, part_rs, res_ss, res_rs, out_ss, out_rs,
):
    s = lax.axis_index("section")
    p = lax.axis_index("expert")
    y, x = p // GRID_X, p % GRID_X
    last = SECTIONS - 1

    loads = [
        pltpu.make_async_copy(wg_hbm.at[0], wgu.at[:, pl.ds(0, LANES)], w_sem.at[0]),
        pltpu.make_async_copy(wu_hbm.at[0], wgu.at[:, pl.ds(LANES, LANES)], w_sem.at[1]),
        pltpu.make_async_copy(wd_hbm.at[0], wd.at[pl.ds(0, LANES)], w_sem.at[2]),
    ]
    near = [
        pltpu.make_async_copy(tok_hbm, tok_ref, w_sem.at[3]),
        pltpu.make_async_copy(gain_hbm, gain_ref, w_sem.at[4]),
    ]
    for load in near + loads:
        load.start()

    def row_at(r):
        return (y + r) % GRID_Y

    def in_row(r, act, skip_self):
        base = row_at(r) * GRID_X
        for dx in DX:
            if not (skip_self and r == 0 and dx == 0):
                act(base + (x + dx) % GRID_X, (GRID_Y - r) % GRID_Y)

    def everyone(act, skip_self):
        def one(k, _):
            r = GRID_Y // 2 + ((k + 1) // 2) * (1 - 2 * (k % 2))
            base = ((y + r) % GRID_Y) * GRID_X
            back = (GRID_Y - r) % GRID_Y
            for dx in DX:
                q = base + (x + dx) % GRID_X
                if skip_self and dx == 0:
                    pl.when(q != p)(lambda q=q: act(q, back))
                else:
                    act(q, back)
            return 0

        lax.fori_loop(0, GRID_Y, one, 0)

    def loop(count, body):
        lax.fori_loop(0, count, lambda k, c: (body(k), c)[1], 0)

    def send(src, dst, ss, rs, section, q):
        pltpu.make_async_remote_copy(
            src, dst, ss, rs, device_id=(section, q), device_id_type=MESH
        ).start()

    def drain(ref, sem):
        pltpu.make_async_copy(ref, ref, sem).wait()

    barrier = pltpu.get_barrier_semaphore()

    def greet(section):
        def one(q, r):
            pl.semaphore_signal(barrier, inc=1, device_id=(section, q), device_id_type=MESH)

        return one

    everyone(greet(s), True)
    pl.when(s > 0)(lambda: everyone(greet(s - 1), False))
    pl.when(s < last)(lambda: everyone(greet(s + 1), False))

    names = [ids_ref[0, t] for t in range(TOK)]
    for t in range(TOK):
        rank = jnp.int32(0)
        for earlier in range(t):
            rank = rank + jnp.where(names[earlier] == names[t], 1, 0)
        slot = names[t] * SLOTS + rank + 2 * (p % 8)
        lane = lax.broadcasted_iota(jnp.int32, (1, LANES), 1)
        meta_send[pl.ds(t, 1), :] = jnp.where(lane < 64, slot.astype(jnp.float32), scale_ref[0, t])
    lane = lax.broadcasted_iota(jnp.int32, (2, LANES), 1)
    meta_send[pl.ds(TOK, 2), :] = jnp.where(lane < 64, -1.0, 0.0)
    @pl.when(s > 0)
    def _():
        meta_own[p] = meta_send[...]


    for load in near:
        load.wait()

    @pl.when(s == 1)
    def _():
        def stage(d):
            columns = pl.ds(pl.multiple_of(d * LANES, LANES), LANES)
            tok_stage[d, pl.ds(0, TOK), :] = tok_ref[:, columns].astype(jnp.float32)
            tok_stage[d, pl.ds(TOK, 2), :] = jnp.zeros((2, LANES), jnp.float32)

        loop(PEERS, stage)
        tok_recv[p] = tok_stage[p]

    met = PEERS - 1 + jnp.where(s > 0, PEERS, 0) + jnp.where(s < last, PEERS, 0)
    pl.semaphore_wait(barrier, met)

    @pl.when(s == 0)
    def _():
        everyone(lambda q, r: send(meta_send, meta_init.at[p], meta_ss, meta_rs.at[2], 1, q), False)

    @pl.when(s == 1)
    def _():
        everyone(lambda q, r: send(tok_stage.at[q], tok_recv.at[p], tok_ss, tok_rs, s, q), True)

    late = s >= EARLY
    worker = (x % 2 == 0)

    def moves(q):
        return [
            pltpu.make_async_remote_copy(
                src, dst, move_ss.at[i], move_rs.at[i], device_id=(s, q), device_id_type=MESH
            )
            for i, (src, dst) in enumerate((
                (wg_hbm.at[0], wgu.at[:, pl.ds(2 * LANES, LANES)]),
                (wu_hbm.at[0], wgu.at[:, pl.ds(3 * LANES, LANES)]),
                (wd_hbm.at[0], wd.at[pl.ds(LANES, LANES)]),
            ))
        ]

    @pl.when(s > 0)
    def _():
        everyone(lambda q, r: send(meta_send, meta_own.at[p], meta_ss, meta_rs.at[0], s, q), True)

    @pl.when(late)
    def _():
        everyone(lambda q, r: send(meta_send, meta_next.at[p], meta_ss, meta_rs.at[1], s - 1, q), False)

    @pl.when(late & jnp.logical_not(worker))
    def _():
        aim = jnp.where(s % 2 == 0, x - 1, (x + 1) % GRID_X)
        for move in moves(y * GRID_X + aim):
            move.start()

    def places(meta, place):
        for m in range(PARTS):
            along = jnp.transpose(meta[8 * m:8 * m + 8].reshape(64, LANES))[:64, :]
            wanted = lax.broadcasted_iota(jnp.int32, (64, 64), 0).astype(jnp.float32)
            place[m] = jnp.where(along == wanted, 1.0, 0.0).astype(jnp.bfloat16)

    def emit(m, rows, place, staged, res, section):
        slotted = jnp.dot(place[m], rows, preferred_element_type=jnp.float32).astype(jnp.bfloat16)
        for e in range(EXPERTS):
            staged[m, e] = slotted[e * SLOTS:(e + 1) * SLOTS]
        everyone(
            lambda q, r: pl.when((section < EARLY) | (q % 2 == 0))(
                lambda: send(
                    staged.at[m, q // 8], disp_recv.at[m, p], disp_ss, disp_rs.at[m, r], section, q
                )
            ),
            False,
        )
        res[m] = rows
        early = section < EARLY
        keeper = jnp.where(early, p, y * GRID_X + 2 * (x // 2) + 1)
        send(
            res.at[m], res_recv.at[m, jnp.where(early, 0, x % 2)], res_ss, res_rs.at[m], section, keeper
        )

    @pl.when(s == 1)
    def _():
        drain(meta_init, meta_rs.at[2])
        places(meta_init, place_init)
        drain(tok_recv.at[pl.ds(0, PEERS - 1)], tok_rs)

        def first(m, _):
            rows = tok_recv[pl.ds(8 * m, 8)].reshape(64, LANES).astype(jnp.bfloat16)
            emit(m, rows, place_init, init_send, res_init, 0)
            return 0

        lax.fori_loop(0, PARTS, first, 0)

    pl.when(s == 1)(lambda: send(meta_init, meta_own, meta_ss, meta_rs.at[0], 0, p))

    @pl.when(s > 0)
    def _():
        drain(meta_own.at[pl.ds(0, PEERS - 1)], meta_rs.at[0])

    pl.when(s == 1)(lambda: send(meta_own, meta_next, meta_ss, meta_rs.at[1], 0, p))

    pl.when(s == 0)(lambda: drain(meta_own, meta_rs.at[0]))
    for m in range(PARTS):
        rows = meta_own[8 * m:8 * m + 8].reshape(64, LANES)
        lane = (lax.broadcasted_iota(jnp.int32, (64, LANES), 1) % 64).astype(jnp.float32)
        chosen[m] = jnp.where(jnp.broadcast_to(rows[:, 0:1], (64, LANES)) == lane, 1.0, 0.0).astype(jnp.bfloat16)
        scales[m] = jnp.broadcast_to(rows[:, 64:65], (64, LANES))

    @pl.when(s < last)
    def _():
        drain(meta_next, meta_rs.at[1])
        places(meta_next, place_next)

        def join(m):
            hop[m] = jnp.dot(place_next[m], chosen[m], preferred_element_type=jnp.float32).astype(jnp.bfloat16)
            hop_scale[m] = jnp.dot(
                place_next[m].astype(jnp.float32), scales[m],
                preferred_element_type=jnp.float32, precision=lax.Precision.HIGHEST,
            )

        loop(PARTS, join)

    def spread(d):
        columns = pl.ds(pl.multiple_of(d * LANES, LANES), LANES)
        gains[d] = jnp.broadcast_to(gain_ref[0:1, columns], (SLOTS, LANES))

    loop(PEERS, spread)
    for load in loads:
        load.wait()

    def row_columns(row):
        return pl.ds(pl.multiple_of(row * GRID_X * LANES, GRID_X * LANES), GRID_X * LANES)

    def work(m, blocks):
        total = jnp.zeros((SLOTS, LANES), jnp.float32)
        acc = jnp.zeros((SLOTS, 2 * blocks * LANES), jnp.float32)
        for group in ARRIVALS:
            for r in group:
                drain(disp_recv.at[m, pl.ds(row_at(r) * GRID_X, GRID_X)], disp_rs.at[m, r])
            for r in group:
                row = row_at(r)
                four = pl.ds(row * GRID_X, GRID_X)
                values = disp_recv[m, four].astype(jnp.float32)
                gained = (values * gains[four]).astype(jnp.bfloat16)
                for c in range(GRID_X):
                    total = total + values[c] * values[c]
                acc = acc + jnp.dot(
                    jnp.concatenate([gained[c] for c in range(GRID_X)], axis=1),
                    wgu[row_columns(row), pl.ds(0, 2 * blocks * LANES)],
                    preferred_element_type=jnp.float32,
                )
        inverse = lax.rsqrt(jnp.sum(total, axis=1, keepdims=True) * (1.0 / (PEERS * LANES)) + 1e-6)
        hidden = []
        for b in range(blocks):
            gate = acc[:, 2 * b * LANES:(2 * b + 1) * LANES] * inverse
            upward = acc[:, (2 * b + 1) * LANES:(2 * b + 2) * LANES] * inverse
            hidden.append((gate / (1.0 + jnp.exp(-gate)) * upward).astype(jnp.bfloat16))
        hidden = jnp.concatenate(hidden, axis=1)
        for group in LEAVING:
            for r in group:
                row = row_at(r)
                part = jnp.dot(
                    hidden, wd[pl.ds(0, blocks * LANES), row_columns(row)], preferred_element_type=jnp.float32
                ).astype(jnp.bfloat16)
                for c in range(GRID_X):
                    part_send[m, row * GRID_X + c] = part[:, c * LANES:(c + 1) * LANES]
            for r in group:
                if blocks == 1:
                    in_row(
                        r,
                        lambda q, r: send(
                            part_send.at[m, q], part_recv.at[m, p], part_ss, part_rs.at[m, r], s, q
                        ),
                        True,
                    )
                else:
                    row = row_at(r)
                    for j in range(2):
                        send(
                            part_send.at[m, pl.ds(row * GRID_X + 2 * j, PAIR)], part_recv.at[m, pl.ds(p, PAIR)],
                            part_ss, part_rs.at[m, (GRID_Y - r) % GRID_Y], s, row * GRID_X + 2 * j + 1,
                        )
        if blocks == 1:
            part_recv[m, p] = part_send[m, p]

    def keep(m):
        drain(res_recv.at[m], res_rs.at[m])

        @pl.when(s < last)
        def _():
            for h in range(PAIR):
                placed[h] = jnp.dot(place_next[m], res_recv[m, h], preferred_element_type=jnp.float32)

        for group in ARRIVALS:
            for r in group:
                drain(part_recv.at[m, pl.ds(row_at(r) * GRID_X, GRID_X)], part_rs.at[m, r])
            for r in group:
                row = row_at(r)
                values = part_recv[m, pl.ds(row * GRID_X, GRID_X)].astype(jnp.float32)
                pair_sums[row] = values[0:2] + values[2:4]
        summed = []
        for h in range(PAIR):
            summed.append(
                jnp.concatenate([pair_sums[2 * e, h] + pair_sums[2 * e + 1, h] for e in range(EXPERTS)], axis=0)
            )
        summed = jnp.concatenate(summed, axis=1)
        high = summed.astype(jnp.bfloat16)
        low = (summed - high.astype(jnp.float32)).astype(jnp.bfloat16)
        both = jnp.concatenate([high, low], axis=0)

        @pl.when(s < last)
        def _():
            moved = jnp.dot(hop[m], both, preferred_element_type=jnp.float32)
            for h in range(PAIR):
                slotted = placed[h] + hop_scale[m] * moved[:, h * LANES:(h + 1) * LANES]
                slotted = slotted.astype(jnp.bfloat16)
                for e in range(EXPERTS):
                    pair_send[m, e, h] = slotted[e * SLOTS:(e + 1) * SLOTS]
            for r in FAR_FIRST:
                row = row_at(r)
                for j in range(2):
                    send(
                        pair_send.at[m, row // 2], disp_recv.at[m, pl.ds(p - 1, PAIR)],
                        disp_ss, disp_rs.at[m, (GRID_Y - r) % GRID_Y], s + 1, row * GRID_X + 2 * j,
                    )

        expert_out = jnp.dot(chosen[m], both, preferred_element_type=jnp.float32)
        before = jnp.concatenate([res_recv[m, h] for h in range(PAIR)], axis=1).astype(jnp.float32)
        scale = jnp.concatenate([scales[m]] * PAIR, axis=1)
        rows = (before + scale * expert_out).astype(jnp.bfloat16)

        @pl.when(s < last)
        def _():
            for h in range(PAIR):
                pair_res[m, h] = rows[:, h * LANES:(h + 1) * LANES]
            send(pair_res.at[m], res_recv.at[m], res_ss, res_rs.at[m], s + 1, p)

        shown = rows.astype(jnp.float32)
        for h in range(PAIR):
            pair_out[m, :, h] = shown[:, h * LANES:(h + 1) * LANES].reshape(8, 8, LANES)
        pl.when(s == last)(lambda: deliver_pair(m))

    def deliver_pair(m):
        mine = pl.ds(p - 1, PAIR)

        def one(j):
            q = 8 * m + j
            pl.when(q != p)(lambda: send(pair_out.at[m, j], out_recv.at[mine], out_ss, out_rs, s, q))

            @pl.when(q == p)
            def _():
                out_recv[mine] = pair_out[m, j]

        loop(8, one)

    def deliver(m):
        for j in range(8):
            q = 8 * m + j

            @pl.when(q != p)
            def _():
                send(out_send.at[m, j], out_recv.at[p], out_ss, out_rs, s, q)

            @pl.when(q == p)
            def _():
                out_recv[p] = out_send[m, j]

    def own(m):
        drain(res_recv.at[m, 0], res_rs.at[m])
        for r in NEAR_FIRST:
            row = row_at(r)
            count = GRID_X - 1 if r == 0 else GRID_X
            drain(part_recv.at[m, pl.ds(row * GRID_X, count)], part_rs.at[m, r])
            four = part_recv[m, pl.ds(row * GRID_X, GRID_X)].astype(jnp.float32)
            row_sums[row] = (four[0] + four[1]) + (four[2] + four[3])
        summed = [row_sums[2 * e] + row_sums[2 * e + 1] for e in range(EXPERTS)]
        summed = jnp.concatenate(summed, axis=0)
        high = summed.astype(jnp.bfloat16)
        low = (summed - high.astype(jnp.float32)).astype(jnp.bfloat16)
        expert_out = jnp.dot(
            chosen[m], jnp.concatenate([high, low], axis=0), preferred_element_type=jnp.float32
        )
        rows = (res_recv[m, 0].astype(jnp.float32) + scales[m] * expert_out).astype(jnp.bfloat16)
        pl.when(s < last)(lambda: emit(m, rows, place_next, disp_send, res_send, s + 1))
        out_send[m] = rows.astype(jnp.float32).reshape(8, 8, LANES)
    @pl.when(s < EARLY)
    def _():
        def step(i):
            pl.when(i < PARTS)(lambda: work(i, 1))
            pl.when(i >= LAG)(lambda: own(i - LAG))

        loop(PARTS + LAG, step)
        loop(PARTS, deliver)

    @pl.when(late & worker)
    def _():
        for move in moves(p):
            move.wait_recv()
        loop(PARTS, lambda m: work(m, 2))

    @pl.when(late & jnp.logical_not(worker))
    def _():
        loop(PARTS, keep)

        @pl.when(s < last)
        def _():
            loop(PARTS, deliver_pair)

        for move in moves(p):
            move.wait_send()

    pl.when(s < EARLY)(lambda: drain(out_recv.at[pl.ds(0, PEERS - 1)], out_rs))
    pl.when(late & worker)(lambda: drain(out_recv, out_rs))
    pl.when(late & jnp.logical_not(worker))(lambda: drain(out_recv.at[pl.ds(0, PEERS - PAIR)], out_rs))

    def store(d):
        columns = pl.ds(pl.multiple_of(d * LANES, LANES), LANES)
        out_ref[0, :, columns] = out_recv[d, 0:TOK, :].astype(jnp.bfloat16)

    loop(PEERS, store)

    drain(meta_own, meta_ss)
    pl.when(s > 0)(lambda: drain(meta_own.at[pl.ds(0, PEERS - 1)], meta_ss))
    pl.when(s == 1)(lambda: drain(meta_own, meta_ss))

    half = PEERS // 2

    @pl.when(s == 0)
    def _():
        drain(disp_recv, disp_ss)
        drain(res_recv.at[:, 0], res_ss)

    @pl.when(s == 1)
    def _():
        drain(tok_recv.at[pl.ds(0, PEERS - 1)], tok_ss)
        drain(disp_recv, disp_ss)
        drain(disp_recv.at[:, pl.ds(0, half)], disp_ss)
        drain(res_recv, res_ss)

    @pl.when(s < EARLY)
    def _():
        drain(part_recv.at[:, pl.ds(0, PEERS - 1)], part_ss)
        drain(out_recv.at[pl.ds(0, PEERS - 1)], out_ss)

    pl.when(late & worker)(lambda: drain(part_recv, part_ss))

    @pl.when(late & jnp.logical_not(worker))
    def _():
        drain(out_recv, out_ss)
        drain(out_recv.at[pl.ds(0, PEERS - PAIR)], out_ss)

        @pl.when(s < last)
        def _():
            drain(disp_recv, disp_ss)
            drain(res_recv, res_ss)


def local(tokens, expert_ids, gate_scale, norm_gain, w_gate, w_up, w_down):
    width = tokens.shape[1]
    vmem = pl.BlockSpec(memory_space=pltpu.VMEM)
    smem = pl.BlockSpec(memory_space=pltpu.SMEM)
    hbm = pl.BlockSpec(memory_space=pltpu.HBM)
    b16, f32 = jnp.bfloat16, jnp.float32
    dma = pltpu.SemaphoreType.DMA
    return pl.pallas_call(
        kernel,
        out_shape=jax.ShapeDtypeStruct((1, TOK, width), b16),
        in_specs=[hbm, smem, smem, hbm, hbm, hbm, hbm],
        out_specs=vmem,
        scratch_shapes=[
            pltpu.VMEM((width, 4 * LANES), b16),
            pltpu.VMEM((2 * LANES, width), b16),
            pltpu.VMEM((TOK, width), b16),
            pltpu.VMEM((1, width), f32),
            pltpu.VMEM((PEERS, 8, LANES), f32),
            pltpu.VMEM((PEERS, 8, LANES), f32),
            pltpu.VMEM((8, LANES), f32),
            pltpu.VMEM((PEERS, 8, LANES), f32),
            pltpu.VMEM((PEERS, 8, LANES), f32),
            pltpu.VMEM((PEERS, 8, LANES), f32),
            pltpu.VMEM((PARTS, 64, 64), b16),
            pltpu.VMEM((PARTS, 64, 64), b16),
            pltpu.VMEM((PARTS, 64, LANES), b16),
            pltpu.VMEM((PARTS, 64, LANES), f32),
            pltpu.VMEM((PARTS, EXPERTS, SLOTS, LANES), b16),
            pltpu.VMEM((PARTS, PEERS, SLOTS, LANES), b16),
            pltpu.VMEM((PARTS, EXPERTS, SLOTS, LANES), b16),
            pltpu.VMEM((PARTS, PEERS, SLOTS, LANES), b16),
            pltpu.VMEM((PARTS, PEERS, SLOTS, LANES), b16),
            pltpu.VMEM((PARTS, 64, LANES), b16),
            pltpu.VMEM((PARTS, 64, LANES), b16),
            pltpu.VMEM((PARTS, PAIR, 64, LANES), b16),
            pltpu.VMEM((PARTS, 8, 8, LANES), f32),
            pltpu.VMEM((PEERS, 8, LANES), f32),
            pltpu.VMEM((PEERS, SLOTS, LANES), f32),
            pltpu.VMEM((GRID_Y, SLOTS, LANES), f32),
            pltpu.VMEM((GRID_Y, PAIR, SLOTS, LANES), f32),
            pltpu.VMEM((PARTS, EXPERTS, PAIR, SLOTS, LANES), b16),
            pltpu.VMEM((PARTS, PAIR, 64, LANES), b16),
            pltpu.VMEM((PARTS, 8, PAIR, 8, LANES), f32),
            pltpu.VMEM((PARTS, 64, LANES), b16),
            pltpu.VMEM((PARTS, 64, LANES), f32),
            pltpu.VMEM((PAIR, 64, LANES), f32),
            dma((5,)),
            dma((3,)),
            dma((3,)),
            dma,
            dma((3,)),
            dma,
            dma,
            dma,
            dma((PARTS, GRID_Y)),
            dma,
            dma((PARTS, GRID_Y)),
            dma,
            dma((PARTS,)),
            dma,
            dma,
        ],
        compiler_params=pltpu.CompilerParams(
            collective_id=0, has_side_effects=True, vmem_limit_bytes=60 * 2**20
        ),
    )(tokens, expert_ids[:, :, 0], gate_scale, norm_gain, w_gate, w_up, w_down)


def solution(mesh):
    return jax.shard_map(
        local,
        mesh=mesh,
        in_specs=(
            P("expert", None),
            P("section", "expert", None),
            P("section", "expert"),
            P("section", None),
            P("section", None, "expert"),
            P("section", None, "expert"),
            P("section", "expert", None),
        ),
        out_specs=P("section", "expert", None),
        check_vma=False,
    )
```

```python
import jax
import jax.numpy as jnp
from jax import lax
from jax.experimental import pallas as pl
from jax.experimental.pallas import tpu as pltpu
from jax.sharding import PartitionSpec as P

MESH = pl.DeviceIdType.MESH
EXPERTS = 4
LANES = 128
PARTS = 4
SLOTS = 16
LAG = 2
GRID_Y, GRID_X = 8, 4
PEERS = GRID_Y * GRID_X
SECTIONS = 16
TOK = 6
PAIR = 2
EARLY = 2
DX = (2, 1, 3, 0)
FAR_FIRST = (4, 3, 5, 2, 6, 1, 7, 0)
ARRIVALS = ((0, 1, 7), (2, 6), (3, 5), (4,))
LEAVING = ((4,), (3, 5, 2, 6), (1, 7, 0))
NEAR_FIRST = (0, 1, 7, 2, 6, 3, 5, 4)


def kernel(
    tok_hbm, ids_ref, scale_ref, gain_hbm, wg_hbm, wu_hbm, wd_hbm, out_ref,
    wgu, wd, tok_ref, gain_ref, tok_stage, tok_recv, meta_send, meta_own, meta_next, meta_init, place_next, place_init, chosen, scales,
    disp_send, disp_recv, init_send, part_send, part_recv, res_send, res_init, res_recv, out_send, out_recv, gains, row_sums,
    pair_sums, pair_send, pair_res, pair_out, hop, hop_scale, placed,
    w_sem, move_ss, move_rs, meta_ss, meta_rs, tok_ss, tok_rs, disp_ss, disp_rs, part_ss, part_rs, res_ss, res_rs, out_ss, out_rs,
):
    s = lax.axis_index("section")
    p = lax.axis_index("expert")
    y, x = p // GRID_X, p % GRID_X
    last = SECTIONS - 1

    loads = [
        pltpu.make_async_copy(wg_hbm.at[0], wgu.at[:, pl.ds(0, LANES)], w_sem.at[0]),
        pltpu.make_async_copy(wu_hbm.at[0], wgu.at[:, pl.ds(LANES, LANES)], w_sem.at[1]),
        pltpu.make_async_copy(wd_hbm.at[0], wd.at[pl.ds(0, LANES)], w_sem.at[2]),
    ]
    near = [
        pltpu.make_async_copy(tok_hbm, tok_ref, w_sem.at[3]),
        pltpu.make_async_copy(gain_hbm, gain_ref, w_sem.at[4]),
    ]
    for load in near + loads:
        load.start()

    def row_at(r):
        return (y + r) % GRID_Y

    def in_row(r, act, skip_self):
        base = row_at(r) * GRID_X
        for dx in DX:
            if not (skip_self and r == 0 and dx == 0):
                act(base + (x + dx) % GRID_X, (GRID_Y - r) % GRID_Y)

    def everyone(act, skip_self):
        def one(k, _):
            r = GRID_Y // 2 + ((k + 1) // 2) * (1 - 2 * (k % 2))
            base = ((y + r) % GRID_Y) * GRID_X
            back = (GRID_Y - r) % GRID_Y
            for dx in DX:
                q = base + (x + dx) % GRID_X
                if skip_self and dx == 0:
                    pl.when(q != p)(lambda q=q: act(q, back))
                else:
                    act(q, back)
            return 0

        lax.fori_loop(0, GRID_Y, one, 0)

    def loop(count, body):
        lax.fori_loop(0, count, lambda k, c: (body(k), c)[1], 0)

    def send(src, dst, ss, rs, section, q):
        pltpu.make_async_remote_copy(
            src, dst, ss, rs, device_id=(section, q), device_id_type=MESH
        ).start()

    def drain(ref, sem):
        pltpu.make_async_copy(ref, ref, sem).wait()

    barrier = pltpu.get_barrier_semaphore()

    def greet(section):
        def one(q, r):
            pl.semaphore_signal(barrier, inc=1, device_id=(section, q), device_id_type=MESH)

        return one

    everyone(greet(s), True)
    pl.when(s > 0)(lambda: everyone(greet(s - 1), False))
    pl.when(s < last)(lambda: everyone(greet(s + 1), False))

    names = [ids_ref[0, t] for t in range(TOK)]
    for t in range(TOK):
        rank = jnp.int32(0)
        for earlier in range(t):
            rank = rank + jnp.where(names[earlier] == names[t], 1, 0)
        slot = names[t] * SLOTS + rank + 2 * (p % 8)
        lane = lax.broadcasted_iota(jnp.int32, (1, LANES), 1)
        meta_send[pl.ds(t, 1), :] = jnp.where(lane < 64, slot.astype(jnp.float32), scale_ref[0, t])
    lane = lax.broadcasted_iota(jnp.int32, (2, LANES), 1)
    meta_send[pl.ds(TOK, 2), :] = jnp.where(lane < 64, -1.0, 0.0)
    @pl.when(s > 0)
    def _():
        meta_own[p] = meta_send[...]


    for load in near:
        load.wait()

    @pl.when(s == 1)
    def _():
        def stage(d):
            columns = pl.ds(pl.multiple_of(d * LANES, LANES), LANES)
            tok_stage[d, pl.ds(0, TOK), :] = tok_ref[:, columns].astype(jnp.float32)
            tok_stage[d, pl.ds(TOK, 2), :] = jnp.zeros((2, LANES), jnp.float32)

        loop(PEERS, stage)
        tok_recv[p] = tok_stage[p]

    met = PEERS - 1 + jnp.where(s > 0, PEERS, 0) + jnp.where(s < last, PEERS, 0)
    pl.semaphore_wait(barrier, met)

    @pl.when(s == 0)
    def _():
        everyone(lambda q, r: send(meta_send, meta_init.at[p], meta_ss, meta_rs.at[2], 1, q), False)

    @pl.when(s == 1)
    def _():
        everyone(lambda q, r: send(tok_stage.at[q], tok_recv.at[p], tok_ss, tok_rs, s, q), True)

    late = s >= EARLY
    worker = (x % 2 == 0)

    def moves(q):
        return [
            pltpu.make_async_remote_copy(
                src, dst, move_ss.at[i], move_rs.at[i], device_id=(s, q), device_id_type=MESH
            )
            for i, (src, dst) in enumerate((
                (wg_hbm.at[0], wgu.at[:, pl.ds(2 * LANES, LANES)]),
                (wu_hbm.at[0], wgu.at[:, pl.ds(3 * LANES, LANES)]),
                (wd_hbm.at[0], wd.at[pl.ds(LANES, LANES)]),
            ))
        ]

    @pl.when(s > 0)
    def _():
        everyone(lambda q, r: send(meta_send, meta_own.at[p], meta_ss, meta_rs.at[0], s, q), True)

    @pl.when(late)
    def _():
        everyone(lambda q, r: send(meta_send, meta_next.at[p], meta_ss, meta_rs.at[1], s - 1, q), False)

    @pl.when(late & jnp.logical_not(worker))
    def _():
        aim = jnp.where(s % 2 == 0, x - 1, (x + 1) % GRID_X)
        for move in moves(y * GRID_X + aim):
            move.start()

    def places(meta, place):
        for m in range(PARTS):
            along = jnp.transpose(meta[8 * m:8 * m + 8].reshape(64, LANES))[:64, :]
            wanted = lax.broadcasted_iota(jnp.int32, (64, 64), 0).astype(jnp.float32)
            place[m] = jnp.where(along == wanted, 1.0, 0.0).astype(jnp.bfloat16)

    def emit(m, rows, place, staged, res, section):
        slotted = jnp.dot(place[m], rows, preferred_element_type=jnp.float32).astype(jnp.bfloat16)
        for e in range(EXPERTS):
            staged[m, e] = slotted[e * SLOTS:(e + 1) * SLOTS]
        everyone(
            lambda q, r: pl.when((section < EARLY) | (q % 2 == 0))(
                lambda: send(
                    staged.at[m, q // 8], disp_recv.at[m, p], disp_ss, disp_rs.at[m, r], section, q
                )
            ),
            False,
        )
        res[m] = rows
        early = section < EARLY
        keeper = jnp.where(early, p, y * GRID_X + 2 * (x // 2) + 1)
        send(
            res.at[m], res_recv.at[m, jnp.where(early, 0, x % 2)], res_ss, res_rs.at[m], section, keeper
        )

    @pl.when(s == 1)
    def _():
        drain(meta_init, meta_rs.at[2])
        places(meta_init, place_init)
        drain(tok_recv.at[pl.ds(0, PEERS - 1)], tok_rs)

        def first(m, _):
            rows = tok_recv[pl.ds(8 * m, 8)].reshape(64, LANES).astype(jnp.bfloat16)
            emit(m, rows, place_init, init_send, res_init, 0)
            return 0

        lax.fori_loop(0, PARTS, first, 0)

    pl.when(s == 1)(lambda: send(meta_init, meta_own, meta_ss, meta_rs.at[0], 0, p))

    @pl.when(s > 0)
    def _():
        drain(meta_own.at[pl.ds(0, PEERS - 1)], meta_rs.at[0])

    pl.when(s == 1)(lambda: send(meta_own, meta_next, meta_ss, meta_rs.at[1], 0, p))

    pl.when(s == 0)(lambda: drain(meta_own, meta_rs.at[0]))
    for m in range(PARTS):
        rows = meta_own[8 * m:8 * m + 8].reshape(64, LANES)
        lane = (lax.broadcasted_iota(jnp.int32, (64, LANES), 1) % 64).astype(jnp.float32)
        chosen[m] = jnp.where(jnp.broadcast_to(rows[:, 0:1], (64, LANES)) == lane, 1.0, 0.0).astype(jnp.bfloat16)
        scales[m] = jnp.broadcast_to(rows[:, 64:65], (64, LANES))

    @pl.when(s < last)
    def _():
        drain(meta_next, meta_rs.at[1])
        places(meta_next, place_next)

        def join(m):
            hop[m] = jnp.dot(place_next[m], chosen[m], preferred_element_type=jnp.float32).astype(jnp.bfloat16)
            hop_scale[m] = jnp.dot(
                place_next[m].astype(jnp.float32), scales[m],
                preferred_element_type=jnp.float32, precision=lax.Precision.HIGHEST,
            )

        loop(PARTS, join)

    def spread(d):
        columns = pl.ds(pl.multiple_of(d * LANES, LANES), LANES)
        gains[d] = jnp.broadcast_to(gain_ref[0:1, columns], (SLOTS, LANES))

    loop(PEERS, spread)
    for load in loads:
        load.wait()

    def row_columns(row):
        return pl.ds(pl.multiple_of(row * GRID_X * LANES, GRID_X * LANES), GRID_X * LANES)

    def work(m, blocks):
        total = jnp.zeros((SLOTS, LANES), jnp.float32)
        acc = jnp.zeros((SLOTS, 2 * blocks * LANES), jnp.float32)
        for group in ARRIVALS:
            for r in group:
                drain(disp_recv.at[m, pl.ds(row_at(r) * GRID_X, GRID_X)], disp_rs.at[m, r])
            for r in group:
                row = row_at(r)
                four = pl.ds(row * GRID_X, GRID_X)
                values = disp_recv[m, four].astype(jnp.float32)
                gained = (values * gains[four]).astype(jnp.bfloat16)
                for c in range(GRID_X):
                    total = total + values[c] * values[c]
                acc = acc + jnp.dot(
                    jnp.concatenate([gained[c] for c in range(GRID_X)], axis=1),
                    wgu[row_columns(row), pl.ds(0, 2 * blocks * LANES)],
                    preferred_element_type=jnp.float32,
                )
        inverse = lax.rsqrt(jnp.sum(total, axis=1, keepdims=True) * (1.0 / (PEERS * LANES)) + 1e-6)
        hidden = []
        for b in range(blocks):
            gate = acc[:, 2 * b * LANES:(2 * b + 1) * LANES] * inverse
            upward = acc[:, (2 * b + 1) * LANES:(2 * b + 2) * LANES] * inverse
            hidden.append((gate / (1.0 + jnp.exp(-gate)) * upward).astype(jnp.bfloat16))
        hidden = jnp.concatenate(hidden, axis=1)
        for group in LEAVING:
            for r in group:
                row = row_at(r)
                part = jnp.dot(
                    hidden, wd[pl.ds(0, blocks * LANES), row_columns(row)], preferred_element_type=jnp.float32
                ).astype(jnp.bfloat16)
                for c in range(GRID_X):
                    part_send[m, row * GRID_X + c] = part[:, c * LANES:(c + 1) * LANES]
            for r in group:
                if blocks == 1:
                    in_row(
                        r,
                        lambda q, r: send(
                            part_send.at[m, q], part_recv.at[m, p], part_ss, part_rs.at[m, r], s, q
                        ),
                        True,
                    )
                else:
                    row = row_at(r)
                    for j in range(2):
                        send(
                            part_send.at[m, pl.ds(row * GRID_X + 2 * j, PAIR)], part_recv.at[m, pl.ds(p, PAIR)],
                            part_ss, part_rs.at[m, (GRID_Y - r) % GRID_Y], s, row * GRID_X + 2 * j + 1,
                        )
        if blocks == 1:
            part_recv[m, p] = part_send[m, p]

    def keep(m):
        drain(res_recv.at[m], res_rs.at[m])

        @pl.when(s < last)
        def _():
            for h in range(PAIR):
                placed[h] = jnp.dot(place_next[m], res_recv[m, h], preferred_element_type=jnp.float32)

        for group in (NEAR_FIRST,):
            for r in group:
                drain(part_recv.at[m, pl.ds(row_at(r) * GRID_X, GRID_X)], part_rs.at[m, r])
            for r in group:
                row = row_at(r)
                values = part_recv[m, pl.ds(row * GRID_X, GRID_X)].astype(jnp.float32)
                pair_sums[row] = values[0:2] + values[2:4]
        summed = []
        for h in range(PAIR):
            summed.append(
                jnp.concatenate([pair_sums[2 * e, h] + pair_sums[2 * e + 1, h] for e in range(EXPERTS)], axis=0)
            )
        summed = jnp.concatenate(summed, axis=1)
        high = summed.astype(jnp.bfloat16)
        low = (summed - high.astype(jnp.float32)).astype(jnp.bfloat16)
        both = jnp.concatenate([high, low], axis=0)

        @pl.when(s < last)
        def _():
            moved = jnp.dot(hop[m], both, preferred_element_type=jnp.float32)
            for h in range(PAIR):
                slotted = placed[h] + hop_scale[m] * moved[:, h * LANES:(h + 1) * LANES]
                slotted = slotted.astype(jnp.bfloat16)
                for e in range(EXPERTS):
                    pair_send[m, e, h] = slotted[e * SLOTS:(e + 1) * SLOTS]
            for r in FAR_FIRST:
                row = row_at(r)
                for j in range(2):
                    send(
                        pair_send.at[m, row // 2], disp_recv.at[m, pl.ds(p - 1, PAIR)],
                        disp_ss, disp_rs.at[m, (GRID_Y - r) % GRID_Y], s + 1, row * GRID_X + 2 * j,
                    )

        expert_out = jnp.dot(chosen[m], both, preferred_element_type=jnp.float32)
        before = jnp.concatenate([res_recv[m, h] for h in range(PAIR)], axis=1).astype(jnp.float32)
        scale = jnp.concatenate([scales[m]] * PAIR, axis=1)
        rows = (before + scale * expert_out).astype(jnp.bfloat16)

        @pl.when(s < last)
        def _():
            for h in range(PAIR):
                pair_res[m, h] = rows[:, h * LANES:(h + 1) * LANES]
            send(pair_res.at[m], res_recv.at[m], res_ss, res_rs.at[m], s + 1, p)

        shown = rows.astype(jnp.float32)
        for h in range(PAIR):
            pair_out[m, :, h] = shown[:, h * LANES:(h + 1) * LANES].reshape(8, 8, LANES)
        pl.when(s == last)(lambda: deliver_pair(m))

    def deliver_pair(m):
        mine = pl.ds(p - 1, PAIR)

        def one(j):
            q = 8 * m + j
            pl.when(q != p)(lambda: send(pair_out.at[m, j], out_recv.at[mine], out_ss, out_rs, s, q))

            @pl.when(q == p)
            def _():
                out_recv[mine] = pair_out[m, j]

        loop(8, one)

    def deliver(m):
        for j in range(8):
            q = 8 * m + j

            @pl.when(q != p)
            def _():
                send(out_send.at[m, j], out_recv.at[p], out_ss, out_rs, s, q)

            @pl.when(q == p)
            def _():
                out_recv[p] = out_send[m, j]

    def own(m):
        drain(res_recv.at[m, 0], res_rs.at[m])
        for r in NEAR_FIRST:
            row = row_at(r)
            count = GRID_X - 1 if r == 0 else GRID_X
            drain(part_recv.at[m, pl.ds(row * GRID_X, count)], part_rs.at[m, r])
            four = part_recv[m, pl.ds(row * GRID_X, GRID_X)].astype(jnp.float32)
            row_sums[row] = (four[0] + four[1]) + (four[2] + four[3])
        summed = [row_sums[2 * e] + row_sums[2 * e + 1] for e in range(EXPERTS)]
        summed = jnp.concatenate(summed, axis=0)
        high = summed.astype(jnp.bfloat16)
        low = (summed - high.astype(jnp.float32)).astype(jnp.bfloat16)
        expert_out = jnp.dot(
            chosen[m], jnp.concatenate([high, low], axis=0), preferred_element_type=jnp.float32
        )
        rows = (res_recv[m, 0].astype(jnp.float32) + scales[m] * expert_out).astype(jnp.bfloat16)
        pl.when(s < last)(lambda: emit(m, rows, place_next, disp_send, res_send, s + 1))
        out_send[m] = rows.astype(jnp.float32).reshape(8, 8, LANES)
    @pl.when(s < EARLY)
    def _():
        def step(i):
            pl.when(i < PARTS)(lambda: work(i, 1))
            pl.when(i >= LAG)(lambda: own(i - LAG))

        loop(PARTS + LAG, step)
        loop(PARTS, deliver)

    @pl.when(late & worker)
    def _():
        for move in moves(p):
            move.wait_recv()
        loop(PARTS, lambda m: work(m, 2))

    @pl.when(late & jnp.logical_not(worker))
    def _():
        loop(PARTS, keep)

        @pl.when(s < last)
        def _():
            loop(PARTS, deliver_pair)

        for move in moves(p):
            move.wait_send()

    pl.when(s < EARLY)(lambda: drain(out_recv.at[pl.ds(0, PEERS - 1)], out_rs))
    pl.when(late & worker)(lambda: drain(out_recv, out_rs))
    pl.when(late & jnp.logical_not(worker))(lambda: drain(out_recv.at[pl.ds(0, PEERS - PAIR)], out_rs))

    def store(d):
        columns = pl.ds(pl.multiple_of(d * LANES, LANES), LANES)
        out_ref[0, :, columns] = out_recv[d, 0:TOK, :].astype(jnp.bfloat16)

    loop(PEERS, store)

    drain(meta_own, meta_ss)
    pl.when(s > 0)(lambda: drain(meta_own.at[pl.ds(0, PEERS - 1)], meta_ss))
    pl.when(s == 1)(lambda: drain(meta_own, meta_ss))

    half = PEERS // 2

    @pl.when(s == 0)
    def _():
        drain(disp_recv, disp_ss)
        drain(res_recv.at[:, 0], res_ss)

    @pl.when(s == 1)
    def _():
        drain(tok_recv.at[pl.ds(0, PEERS - 1)], tok_ss)
        drain(disp_recv, disp_ss)
        drain(disp_recv.at[:, pl.ds(0, half)], disp_ss)
        drain(res_recv, res_ss)

    @pl.when(s < EARLY)
    def _():
        drain(part_recv.at[:, pl.ds(0, PEERS - 1)], part_ss)
        drain(out_recv.at[pl.ds(0, PEERS - 1)], out_ss)

    pl.when(late & worker)(lambda: drain(part_recv, part_ss))

    @pl.when(late & jnp.logical_not(worker))
    def _():
        drain(out_recv, out_ss)
        drain(out_recv.at[pl.ds(0, PEERS - PAIR)], out_ss)

        @pl.when(s < last)
        def _():
            drain(disp_recv, disp_ss)
            drain(res_recv, res_ss)


def local(tokens, expert_ids, gate_scale, norm_gain, w_gate, w_up, w_down):
    width = tokens.shape[1]
    vmem = pl.BlockSpec(memory_space=pltpu.VMEM)
    smem = pl.BlockSpec(memory_space=pltpu.SMEM)
    hbm = pl.BlockSpec(memory_space=pltpu.HBM)
    b16, f32 = jnp.bfloat16, jnp.float32
    dma = pltpu.SemaphoreType.DMA
    return pl.pallas_call(
        kernel,
        out_shape=jax.ShapeDtypeStruct((1, TOK, width), b16),
        in_specs=[hbm, smem, smem, hbm, hbm, hbm, hbm],
        out_specs=vmem,
        scratch_shapes=[
            pltpu.VMEM((width, 4 * LANES), b16),
            pltpu.VMEM((2 * LANES, width), b16),
            pltpu.VMEM((TOK, width), b16),
            pltpu.VMEM((1, width), f32),
            pltpu.VMEM((PEERS, 8, LANES), f32),
            pltpu.VMEM((PEERS, 8, LANES), f32),
            pltpu.VMEM((8, LANES), f32),
            pltpu.VMEM((PEERS, 8, LANES), f32),
            pltpu.VMEM((PEERS, 8, LANES), f32),
            pltpu.VMEM((PEERS, 8, LANES), f32),
            pltpu.VMEM((PARTS, 64, 64), b16),
            pltpu.VMEM((PARTS, 64, 64), b16),
            pltpu.VMEM((PARTS, 64, LANES), b16),
            pltpu.VMEM((PARTS, 64, LANES), f32),
            pltpu.VMEM((PARTS, EXPERTS, SLOTS, LANES), b16),
            pltpu.VMEM((PARTS, PEERS, SLOTS, LANES), b16),
            pltpu.VMEM((PARTS, EXPERTS, SLOTS, LANES), b16),
            pltpu.VMEM((PARTS, PEERS, SLOTS, LANES), b16),
            pltpu.VMEM((PARTS, PEERS, SLOTS, LANES), b16),
            pltpu.VMEM((PARTS, 64, LANES), b16),
            pltpu.VMEM((PARTS, 64, LANES), b16),
            pltpu.VMEM((PARTS, PAIR, 64, LANES), b16),
            pltpu.VMEM((PARTS, 8, 8, LANES), f32),
            pltpu.VMEM((PEERS, 8, LANES), f32),
            pltpu.VMEM((PEERS, SLOTS, LANES), f32),
            pltpu.VMEM((GRID_Y, SLOTS, LANES), f32),
            pltpu.VMEM((GRID_Y, PAIR, SLOTS, LANES), f32),
            pltpu.VMEM((PARTS, EXPERTS, PAIR, SLOTS, LANES), b16),
            pltpu.VMEM((PARTS, PAIR, 64, LANES), b16),
            pltpu.VMEM((PARTS, 8, PAIR, 8, LANES), f32),
            pltpu.VMEM((PARTS, 64, LANES), b16),
            pltpu.VMEM((PARTS, 64, LANES), f32),
            pltpu.VMEM((PAIR, 64, LANES), f32),
            dma((5,)),
            dma((3,)),
            dma((3,)),
            dma,
            dma((3,)),
            dma,
            dma,
            dma,
            dma((PARTS, GRID_Y)),
            dma,
            dma((PARTS, GRID_Y)),
            dma,
            dma((PARTS,)),
            dma,
            dma,
        ],
        compiler_params=pltpu.CompilerParams(
            collective_id=0, has_side_effects=True, vmem_limit_bytes=60 * 2**20
        ),
    )(tokens, expert_ids[:, :, 0], gate_scale, norm_gain, w_gate, w_up, w_down)


def solution(mesh):
    return jax.shard_map(
        local,
        mesh=mesh,
        in_specs=(
            P("expert", None),
            P("section", "expert", None),
            P("section", "expert"),
            P("section", None),
            P("section", None, "expert"),
            P("section", None, "expert"),
            P("section", "expert", None),
        ),
        out_specs=P("section", "expert", None),
        check_vma=False,
    )
```
